256 devices in a mesh: storey: 64 (over z, y, core), inner: 4 (over x).
Axes of the slice: x: 4, y: 4, z: 8, core: 2. Of those that a mesh axis runs over, the one named last changes fastest.
Arguments:
- synthesis: bfloat16 [3072, 3072], P('inner'), may hold values from -0.109375 to 0.109375
- analysis: bfloat16 [3072, 3072], P(None, 'inner'), may hold values from -0.109375 to 0.109375
- pivot: float32 [128, 3072], P('storey', 'inner'), may hold values from 0.1 to 0.4
- transfer: float32 [128, 3072], P('storey', 'inner'), may hold values from -1 to 1, as said below
- displacement: float32 [128, 3072], P('storey', 'inner'), may hold values from -6 to 6
- directions: bfloat16 [3072, 128, 128], P('inner', 'storey'), may hold values from -6 to 6
- sensor_pairs: int32 [128, 512, 2], P('storey'), may hold values from 0 to 3071
- sensor_weights: float32 [128, 512], P('storey'), may hold values from 0.1 to 1
Outputs:
- curvature_product: float32 [3072, 128, 128], P('inner', 'storey')
The draws below stay inside these ranges and needn't reach their ends.
Inputs may be any that keep to these rules, and one draw needn't show every extreme that they name: `sensor_pairs`: each sensor's two degree-of-freedom indices within its storey's interface. `transfer`: magnitudes below one.
All inputs are finite; a program needn't handle non-finite values.
Results may differ from the reference program's by a relative error of at most 0.017.
Values may be sent and summed in bfloat16 or wider, within the bound.
A program may use at most 128 MiB of HBM per device.

```python
import math
import jax
import jax.numpy as jnp
from jax import lax

W = 3072
M = 512
NCOL = 128
LEVEL_TOTAL = 128


def draw_transfer(key, part):
    key = jax.random.fold_in(key, 11)
    stochastic_seed_list = jax.random.split(key, 7)
    slow_share = 0.5
    jitter_reach = 0.35
    slow_mode = jax.random.uniform(stochastic_seed_list[0], (W,)) < slow_share
    whole_loss = jax.random.uniform(stochastic_seed_list[1], (W,), minval=0.1, maxval=0.6)
    fast_reach = jnp.exp(jax.random.uniform(stochastic_seed_list[2], (W,), minval=math.log(3.0), maxval=math.log(12.0)))
    step_loss = jnp.where(slow_mode, whole_loss / LEVEL_TOTAL, 1.0 / fast_reach)
    jitter = jnp.exp(jax.random.uniform(stochastic_seed_list[3], (LEVEL_TOTAL, W), minval=-jitter_reach, maxval=jitter_reach))
    excitation_pulse_entries = jax.random.uniform(stochastic_seed_list[4], (LEVEL_TOTAL, 1)) < 2.5 / LEVEL_TOTAL
    surviving_pulse_train_entries = jax.random.uniform(stochastic_seed_list[5], (LEVEL_TOTAL, 1), minval=0.5, maxval=0.8)
    modal_segment_matrix = jnp.where(excitation_pulse_entries, surviving_pulse_train_entries, 1.0)
    flip_sign = jnp.where(jax.random.uniform(stochastic_seed_list[6], (LEVEL_TOTAL, W)) < 0.5, -1.0, 1.0)
    magnitude = jnp.exp(-step_loss[None, :] * jitter) * modal_segment_matrix
    return (flip_sign * magnitude).astype(jnp.float32)


def place_ends(array, stream_key, low, largest):
    longest = array.shape.index(max(array.shape))
    spots = []
    for shift in (0, 1):
        where = [jax.random.randint(jax.random.fold_in(stream_key, axis), (), 0, length) for axis, length in enumerate(array.shape)]
        where[longest] = (where[longest] + shift) % array.shape[longest]
        spots.append(tuple(where))
    return array.at[spots[0]].set(low).at[spots[1]].set(largest)


def levels(rng, extent, cuts, low, top_value):
    gain = 1.0
    for position, shards_of in cuts:
        draws = jax.random.uniform(jax.random.fold_in(jax.random.fold_in(rng, 6), position), (shards_of,), jnp.float32, low / len(cuts), top_value / len(cuts))
        gain = gain * jnp.repeat(jnp.exp(draws), extent[position] // shards_of).reshape((-1,) + (1,) * (len(extent) - 1 - position))
    return gain


def normal_values(rng, extent, deviation, reach, pieces=(), kind=jnp.bfloat16):
    array = jax.random.normal(rng, extent, jnp.float32) * deviation
    if len(pieces) > 0:
        array = levels(rng, extent, pieces, -0.22, 0.18) * array
    return jnp.clip(array, min=-reach, max=reach).astype(kind)


def setup_inputs(seed: int = 0) -> dict:
    splits = jax.random.split(jax.random.key(seed), 9)
    synthesis = normal_values(splits[0], (W, W), W ** -0.5, 0.109375, ((0, 4),))
    analysis = normal_values(splits[1], (W, W), W ** -0.5, 0.109375, ((1, 4),))
    pivot = jnp.clip(jnp.exp(math.log(0.4) - 1.3862944 * jax.random.uniform(splits[2], (LEVEL_TOTAL, W), jnp.float32) ** levels(splits[2], (LEVEL_TOTAL, W), ((0, 64), (1, 4)), -0.2, 0.2)), 0.1, 0.4)
    transfer = draw_transfer(jax.random.fold_in(splits[8], 71), 0)
    displacement = normal_values(splits[4], (LEVEL_TOTAL, W), 1.0, 6.0, ((0, 64), (1, 4)), jnp.float32)
    directions = normal_values(splits[5], (W, LEVEL_TOTAL, NCOL), 1.0, 6.0, ((0, 4), (1, 64)))
    sensor_pairs = place_ends(jax.random.randint(splits[6], (LEVEL_TOTAL, M, 2), 0, W), jax.random.fold_in(splits[6], 1), 0, W - 1).astype(jnp.int32)
    sensor_weights = jnp.clip(jnp.exp(math.log(1.0) - 2.3025851 * jax.random.uniform(splits[7], (LEVEL_TOTAL, M), jnp.float32) ** levels(splits[7], (LEVEL_TOTAL, M), ((0, 64),), -0.2, 0.2)), 0.1, 1.0)
    return {"synthesis": synthesis, "analysis": analysis, "pivot": pivot, "transfer": transfer, "displacement": displacement, "directions": directions, "sensor_pairs": sensor_pairs, "sensor_weights": sensor_weights}


def reference(synthesis, analysis, pivot, transfer, displacement, directions, sensor_pairs, sensor_weights):
    freedom_count, storeys, columns = directions.shape
    load_scale = displacement.T[:, :, None]
    tangent_load = (-(load_scale * directions.astype(jnp.float32))).astype(jnp.bfloat16)
    modal_load = jnp.dot(analysis, tangent_load.reshape(freedom_count, storeys * columns), preferred_element_type=jnp.float32)
    modal_load = modal_load.reshape(freedom_count, storeys, columns).transpose(1, 0, 2)

    def climb_step(modal_carry, inputs):
        decay_rate, pivot_gain, source_term = inputs
        modal_carry = decay_rate[:, None] * modal_carry + pivot_gain[:, None] * source_term
        return modal_carry, modal_carry

    _, modal_state = lax.scan(climb_step, jnp.zeros((freedom_count, columns), jnp.float32), (transfer, pivot, modal_load))
    modal_round = modal_state.astype(jnp.bfloat16).transpose(1, 0, 2).reshape(freedom_count, storeys * columns)
    tangent = jnp.dot(synthesis, modal_round, preferred_element_type=jnp.float32)
    tangent = tangent.reshape(freedom_count, storeys, columns).transpose(1, 0, 2)
    upper_dof = sensor_pairs[:, :, 0].astype(jnp.int32)
    lower_dof = sensor_pairs[:, :, 1].astype(jnp.int32)
    readings = jnp.take_along_axis(tangent, upper_dof[:, :, None], axis=1) - jnp.take_along_axis(tangent, lower_dof[:, :, None], axis=1)
    weighted = sensor_weights[:, :, None] * readings

    def distribute_storey(first_dof, second_dof, values):
        empty_nodal_vector = jnp.zeros((freedom_count, columns), jnp.float32)
        return empty_nodal_vector.at[first_dof].add(values).at[second_dof].add(-values)

    adjoint_load = jax.vmap(distribute_storey)(upper_dof, lower_dof, weighted)
    adjoint_round = adjoint_load.astype(jnp.bfloat16).transpose(1, 0, 2).reshape(freedom_count, storeys * columns)
    modal_adjoint = jnp.dot(synthesis.T, adjoint_round, preferred_element_type=jnp.float32)
    modal_adjoint = modal_adjoint.reshape(freedom_count, storeys, columns).transpose(1, 0, 2)

    def descend_step(carried, inputs):
        decay_rate, source_term = inputs
        gathered_sum = source_term + carried
        return decay_rate[:, None] * gathered_sum, gathered_sum

    _, gathered = lax.scan(descend_step, jnp.zeros((freedom_count, columns), jnp.float32), (transfer, modal_adjoint), reverse=True)
    weighted_modes = (pivot[:, :, None] * gathered).astype(jnp.bfloat16)
    weighted_modes = weighted_modes.transpose(1, 0, 2).reshape(freedom_count, storeys * columns)
    response = jnp.dot(analysis.T, weighted_modes, preferred_element_type=jnp.float32)
    response = response.reshape(freedom_count, storeys, columns)
    return -load_scale * response
```

```python
import functools

import jax
import jax.numpy as jnp
from jax import lax
from jax.experimental import pallas as pl
from jax.experimental.pallas import tpu as pltpu
from jax.sharding import PartitionSpec as P

MESH = pl.DeviceIdType.MESH
F32 = jnp.float32
BF16 = jnp.bfloat16

NX = 4
NW = 8
NZ = 8
NK = 2

NN = (((1,), (0,)), ((), ()))
NT = (((1,), (1,)), ((), ()))


def mm(a, b, dims):
    return lax.dot_general(a, b, dims, preferred_element_type=F32)


def kernel(
    load_ref, pivot_ref, transfer_ref, disp_ref, pairs_ref, weights_ref, analysis_hbm, synthesis_hbm,
    out_ref,
    A, S, E, acc, part, own, opp_out, opp_in, mid_out, mid_in, src0, src1,
    blk, gath, shift_out, group_in, zone_in, reply, carry,
    rate_group, rate_zone, tang, read_out, read_in, wread, adj,
    a_sem, s_sem, x_send, x_recv, c_send, c_recv, r_send, r_recv, q_send, q_recv,
):
    storey = lax.axis_index("storey")
    x = lax.axis_index("inner")
    z = lax.div(storey, NW)
    w = lax.rem(storey, NW)
    rows, dofs = load_ref.shape
    cols = rows // 2
    mc = dofs // NK
    lane = cols // NW
    right, left, oppo = lax.rem(x + 1, NX), lax.rem(x + 3, NX), lax.rem(x + 2, NX)
    pending = []

    def xdev(i):
        return (storey, i)

    def wdev(i):
        return (z * NW + i, x)

    def zdev(i):
        return (i * NW + w, x)

    def remote(src, dst, ssem, rsem, dev):
        return pltpu.make_async_remote_copy(
            src_ref=src, dst_ref=dst, send_sem=ssem, recv_sem=rsem, device_id=dev, device_id_type=MESH
        )

    def send(src, dst, ssem, rsem, dev):
        c = remote(src, dst, ssem, rsem, dev)
        c.start()
        pending.append(c)

    def arrive(dst, ssem, rsem, dev):
        remote(dst, dst, ssem, rsem, dev).wait_recv()

    def mode_at(t, k):
        return pl.multiple_of(t * dofs + k * mc, 128)

    a_copies = {}
    for k in range(NK):
        for j, t in enumerate((oppo, right, left, x)):
            at = pl.ds(mode_at(t, k), mc)
            c = pltpu.make_async_copy(analysis_hbm.at[at, :], A.at[at, :], a_sem.at[k * 4 + j])
            c.start()
            a_copies[(k, j)] = c
    s_copy = pltpu.make_async_copy(synthesis_hbm, S, s_sem.at[0])
    s_copy.start()

    barrier = pltpu.get_barrier_semaphore()
    for d in range(1, NX):
        pl.semaphore_signal(barrier, inc=1, device_id=xdev(lax.rem(x + d, NX)), device_id_type=MESH)
    for d in range(1, NW):
        pl.semaphore_signal(barrier, inc=1, device_id=wdev(lax.rem(w + d, NW)), device_id_type=MESH)
    for d in range(1, NZ):
        pl.semaphore_signal(barrier, inc=1, device_id=zdev(lax.rem(z + d, NZ)), device_id_type=MESH)
    pl.semaphore_wait(barrier, NX + NW + NZ - 3)

    t0 = transfer_ref[0:1, :]
    t1 = transfer_ref[1:2, :]
    rate = t0 * t1

    def rates_first():
        rate_group[w] = jnp.broadcast_to(rate, (8, dofs))
        for d in range(1, NW):
            i = lax.rem(w + d, NW)
            send(rate_group.at[w], rate_group.at[w], r_send.at[0, i], r_recv.at[0, w], wdev(i))

    def rates_second():
        for d in range(1, NW):
            i = lax.rem(w + d, NW)
            arrive(rate_group.at[i], r_send.at[0, i], r_recv.at[0, i], wdev(i))
        total = rate_group[0]
        for i in range(1, NW):
            total = total * rate_group[i]
        rate_zone[z] = total
        for d in range(1, NZ):
            i = lax.rem(z + d, NZ)
            send(rate_zone.at[z], rate_zone.at[z], r_send.at[1, i], r_recv.at[1, z], zdev(i))

    def rates_third():
        for d in range(1, NZ):
            i = lax.rem(z + d, NZ)
            arrive(rate_zone.at[i], r_send.at[1, i], r_recv.at[1, i], zdev(i))

    def project(v, k, t, j):
        if v == 0:
            a_copies[(k, j)].wait()
            return mm(load_ref[...], A[pl.ds(mode_at(t, k), mc), :], NT)
        return mm(adj[...], S[:, pl.ds(mode_at(t, k), mc)], NN)

    def rs_opp(v, k):
        opp_out[v, k] = project(v, k, oppo, 0).astype(BF16).reshape(2, cols, mc)
        send(opp_out.at[v, k, 0], opp_in.at[v, k, 0], x_send.at[v, k, 0], x_recv.at[v, k, 0], xdev(right))
        send(opp_out.at[v, k, 1], opp_in.at[v, k, 1], x_send.at[v, k, 1], x_recv.at[v, k, 1], xdev(left))

    def rs_parts(v, k):
        part[0] = project(v, k, right, 1)
        part[1] = project(v, k, left, 2)

    def rs_mid(v, k):
        arrive(opp_in.at[v, k, 0], x_send.at[v, k, 0], x_recv.at[v, k, 0], xdev(left))
        mid_out[v, k, 0, 0:cols] = (part[0, 0:cols] + opp_in[v, k, 0].astype(F32)).astype(BF16)
        mid_out[v, k, 0, cols:rows] = part[0, cols:rows].astype(BF16)
        send(mid_out.at[v, k, 0], mid_in.at[v, k, 0], x_send.at[v, k, 2], x_recv.at[v, k, 2], xdev(right))
        arrive(opp_in.at[v, k, 1], x_send.at[v, k, 1], x_recv.at[v, k, 1], xdev(right))
        mid_out[v, k, 1, 0:cols] = part[1, 0:cols].astype(BF16)
        mid_out[v, k, 1, cols:rows] = (part[1, cols:rows] + opp_in[v, k, 1].astype(F32)).astype(BF16)
        send(mid_out.at[v, k, 1], mid_in.at[v, k, 1], x_send.at[v, k, 3], x_recv.at[v, k, 3], xdev(left))

    def rs_own(v, k):
        own[k] = project(v, k, x, 3)

    def lanes(k):
        return slice(k * mc, (k + 1) * mc)

    def scan_first(v, k):
        arrive(mid_in.at[v, k, 0], x_send.at[v, k, 2], x_recv.at[v, k, 2], xdev(left))
        arrive(mid_in.at[v, k, 1], x_send.at[v, k, 3], x_recv.at[v, k, 3], xdev(right))
        total = own[k] + mid_in[v, k, 0].astype(F32) + mid_in[v, k, 1].astype(F32)
        low, high = total[0:cols], total[cols:rows]
        if v == 0:
            low = low * pivot_ref[0:1, lanes(k)]
            high = high * pivot_ref[1:2, lanes(k)]
            shift = low * t1[:, lanes(k)] + high
        else:
            shift = low * t0[:, lanes(k)] + high * rate[:, lanes(k)]
        src0[k] = low
        src1[k] = high
        shift_out[v, k] = shift.astype(BF16).reshape(NW, lane, mc)
        for d in range(1, NW):
            i = lax.rem(w + d, NW)
            send(shift_out.at[v, k, i], group_in.at[v, k, w], c_send.at[v, k, 0, i], c_recv.at[v, k, 0, w], wdev(i))
        group_in[v, k, w] = shift_out[v, k, w]

    def order(v, n):
        return range(n) if v == 0 else range(n - 1, -1, -1)

    def scan_second(v, k):
        for d in range(1, NW):
            i = lax.rem(w + d, NW)
            arrive(group_in.at[v, k, i], c_send.at[v, k, 0, i], c_recv.at[v, k, 0, i], wdev(i))
        total = None
        for i in order(v, NW):
            term = group_in[v, k, i].astype(F32)
            total = term if total is None else total * rate_group[i, 0:1, lanes(k)] + term
        zone_in[v, k, z] = total.astype(BF16)
        for d in range(1, NZ):
            i = lax.rem(z + d, NZ)
            send(zone_in.at[v, k, z], zone_in.at[v, k, z], c_send.at[v, k, 1, i], c_recv.at[v, k, 1, z], zdev(i))

    def scan_third(v, k):
        for d in range(1, NZ):
            i = lax.rem(z + d, NZ)
            arrive(zone_in.at[v, k, i], c_send.at[v, k, 1, i], c_recv.at[v, k, 1, i], zdev(i))
        state = jnp.zeros((lane, mc), F32)
        for i in order(v, NZ):
            ahead = (i < z) if v == 0 else (i > z)
            state = jnp.where(ahead, state * rate_zone[i, 0:1, lanes(k)] + zone_in[v, k, i].astype(F32), state)
        for i in order(v, NW):
            reply[v, k, i] = state.astype(BF16)
            state = state * rate_group[i, 0:1, lanes(k)] + group_in[v, k, i].astype(F32)
        for d in range(1, NW):
            i = lax.rem(w + d, NW)
            send(reply.at[v, k, i], carry.at[v, k, w], c_send.at[v, k, 2, i], c_recv.at[v, k, 2, w], wdev(i))
        carry[v, k, w] = reply[v, k, w]

    def ag_first(v, k):
        for d in range(1, NW):
            i = lax.rem(w + d, NW)
            arrive(carry.at[v, k, i], c_send.at[v, k, 2, i], c_recv.at[v, k, 2, i], wdev(i))
        state = carry[v, k].reshape(cols, mc).astype(F32)
        if v == 0:
            low = state * t0[:, lanes(k)] + src0[k]
            high = low * t1[:, lanes(k)] + src1[k]
        else:
            high = src1[k] + state
            low = src0[k] + high * t1[:, lanes(k)]
            low = low * pivot_ref[0:1, lanes(k)]
            high = high * pivot_ref[1:2, lanes(k)]
        blk[v, k, 0:cols] = low.astype(BF16)
        blk[v, k, cols:rows] = high.astype(BF16)
        send(blk.at[v, k], gath.at[v, k, 0], x_send.at[v, k, 4], x_recv.at[v, k, 4], xdev(right))
        send(blk.at[v, k], gath.at[v, k, 1], x_send.at[v, k, 5], x_recv.at[v, k, 5], xdev(left))

    def ag_second(v, k):
        lo, hi = pl.ds(0, cols), pl.ds(cols, cols)
        arrive(gath.at[v, k, 0], x_send.at[v, k, 4], x_recv.at[v, k, 4], xdev(left))
        send(gath.at[v, k, 0, lo], gath.at[v, k, 2, lo], x_send.at[v, k, 6], x_recv.at[v, k, 6], xdev(right))
        arrive(gath.at[v, k, 1], x_send.at[v, k, 5], x_recv.at[v, k, 5], xdev(right))
        send(gath.at[v, k, 1, hi], gath.at[v, k, 2, hi], x_send.at[v, k, 7], x_recv.at[v, k, 7], xdev(left))

    def ag_third(v, k):
        lo, hi = pl.ds(0, cols), pl.ds(cols, cols)
        arrive(gath.at[v, k, 2, lo], x_send.at[v, k, 6], x_recv.at[v, k, 6], xdev(left))
        arrive(gath.at[v, k, 2, hi], x_send.at[v, k, 7], x_recv.at[v, k, 7], xdev(right))

    def expand(v, k, t, val):
        if v == 0:
            return mm(val, S[:, pl.ds(mode_at(t, k), mc)], NT)
        return mm(val, A[pl.ds(mode_at(t, k), mc), :], NN)

    def sweep(v):
        rs_opp(v, 0)
        if v == 0:
            rates_first()
        rs_parts(v, 0)
        rs_mid(v, 0)
        rs_own(v, 0)
        rs_opp(v, 1)
        if v == 0:
            rates_second()
        rs_parts(v, 1)
        scan_first(v, 0)
        rs_mid(v, 1)
        rs_own(v, 1)
        scan_second(v, 0)
        if v == 0:
            rates_third()
            build_incidence()
        scan_third(v, 0)
        scan_first(v, 1)
        ag_first(v, 0)
        scan_second(v, 1)
        if v == 0:
            s_copy.wait()
        acc[...] = expand(v, 0, x, blk[v, 0])
        ag_second(v, 0)
        scan_third(v, 1)
        acc[...] += expand(v, 0, left, gath[v, 0, 0]) + expand(v, 0, right, gath[v, 0, 1])
        ag_first(v, 1)
        ag_third(v, 0)
        acc[...] += expand(v, 0, oppo, gath[v, 0, 2]) + expand(v, 1, x, blk[v, 1])
        ag_second(v, 1)
        acc[...] += expand(v, 1, left, gath[v, 1, 0]) + expand(v, 1, right, gath[v, 1, 1])
        ag_third(v, 1)
        acc[...] += expand(v, 1, oppo, gath[v, 1, 2])

    def build_incidence():
        sensors = pairs_ref.shape[1]
        for s in range(2):
            upper = pairs_ref[2 * s : 2 * s + 1, :] - x * dofs
            lower = pairs_ref[2 * s + 1 : 2 * s + 2, :] - x * dofs
            for b in range(0, dofs, 128):
                ids = lax.broadcasted_iota(jnp.int32, (128, sensors), 0) + b
                e = jnp.where(ids == upper, 1.0, 0.0) - jnp.where(ids == lower, 1.0, 0.0)
                E[s, b : b + 128] = e.astype(BF16)

    sweep(0)

    quarter = rows // NX
    for s in range(2):
        tang[s] = acc[s * cols : (s + 1) * cols].astype(BF16)
        r = mm(tang[s], E[s], NN).astype(BF16)
        read_out[2 * s : 2 * s + 2] = r.reshape(2, quarter, r.shape[-1])
    for d in (2, 1, 3):
        i = lax.rem(x + d, NX)
        send(read_out.at[i], read_in.at[x], q_send.at[0, i], q_recv.at[0, x], xdev(i))
    read_in[x] = read_out[x]
    for d in (1, 3, 2):
        i = lax.rem(x + d, NX)
        arrive(read_in.at[i], q_send.at[0, i], q_recv.at[0, i], xdev(i))
    total = read_in[0].astype(F32)
    for i in range(1, NX):
        total = total + read_in[i].astype(F32)
    weight = weights_ref[pl.ds(lax.div(x, 2), 1), :]
    wread[x] = (total * weight).astype(BF16)
    for d in (2, 1, 3):
        i = lax.rem(x + d, NX)
        send(wread.at[x], wread.at[x], q_send.at[1, i], q_recv.at[1, x], xdev(i))
    for d in (1, 3, 2):
        i = lax.rem(x + d, NX)
        arrive(wread.at[i], q_send.at[1, i], q_recv.at[1, i], xdev(i))
    for s in range(2):
        r = wread[2 * s : 2 * s + 2].reshape(cols, wread.shape[-1])
        adj[s * cols : (s + 1) * cols] = mm(r, E[s], NT).astype(BF16)

    sweep(1)

    for s in range(2):
        at = slice(s * cols, (s + 1) * cols)
        out_ref[at] = -disp_ref[s : s + 1, :] * acc[at]
    for c in pending:
        c.wait_send()


def chain(load, pivot, transfer, disp, pairs, weights, analysis, synthesis):
    rows, dofs = load.shape
    modes = analysis.shape[0]
    cols = rows // 2
    mc = dofs // NK
    lane = cols // NW
    sensors = pairs.shape[1]
    vm = pltpu.VMEM
    dma = pltpu.SemaphoreType.DMA
    scratch = [
        vm((modes, dofs), BF16),
        vm((dofs, modes), BF16),
        vm((2, dofs, sensors), BF16),
        vm((rows, dofs), F32),
        vm((2, rows, mc), F32),
        vm((NK, rows, mc), F32),
        vm((2, NK, 2, cols, mc), BF16),
        vm((2, NK, 2, cols, mc), BF16),
        vm((2, NK, 2, rows, mc), BF16),
        vm((2, NK, 2, rows, mc), BF16),
        vm((NK, cols, mc), F32),
        vm((NK, cols, mc), F32),
        vm((2, NK, rows, mc), BF16),
        vm((2, NK, 3, rows, mc), BF16),
        vm((2, NK, NW, lane, mc), BF16),
        vm((2, NK, NW, lane, mc), BF16),
        vm((2, NK, NZ, lane, mc), BF16),
        vm((2, NK, NW, lane, mc), BF16),
        vm((2, NK, NW, lane, mc), BF16),
        vm((NW, 8, dofs), F32),
        vm((NZ, 8, dofs), F32),
        vm((2, cols, dofs), BF16),
        vm((NX, rows // NX, sensors), BF16),
        vm((NX, rows // NX, sensors), BF16),
        vm((NX, rows // NX, sensors), BF16),
        vm((rows, dofs), BF16),
        dma((8,)), dma((1,)),
        dma((2, NK, 8)), dma((2, NK, 8)),
        dma((2, NK, 3, 8)), dma((2, NK, 3, 8)),
        dma((2, 8)), dma((2, 8)),
        dma((2, 4)), dma((2, 4)),
    ]
    in_vmem = pl.BlockSpec(memory_space=pltpu.VMEM)
    in_hbm = pl.BlockSpec(memory_space=pl.ANY)
    return pl.pallas_call(
        kernel,
        out_shape=jax.ShapeDtypeStruct((rows, dofs), F32),
        in_specs=[in_vmem] * 6 + [in_hbm] * 2,
        out_specs=in_vmem,
        scratch_shapes=scratch,
        compiler_params=pltpu.CompilerParams(
            collective_id=0, has_side_effects=True, vmem_limit_bytes=56 * 1024 * 1024
        ),
        cost_estimate=pl.CostEstimate(
            flops=8 * rows * modes * dofs, bytes_accessed=4 * modes * dofs, transcendentals=0
        ),
        name="chain",
    )(load, pivot, transfer, disp, pairs, weights, analysis, synthesis)


def local(synthesis, analysis, pivot, transfer, displacement, directions, sensor_pairs, sensor_weights):
    dofs, storeys, columns = directions.shape
    load = (-(displacement.T[:, :, None] * directions.astype(F32))).astype(BF16)
    load = load.transpose(1, 2, 0).reshape(storeys * columns, dofs)
    pairs = sensor_pairs.transpose(0, 2, 1).reshape(2 * storeys, -1)
    out = chain(load, pivot, transfer, displacement, pairs, sensor_weights, analysis, synthesis)
    return out.reshape(storeys, columns, dofs).transpose(2, 0, 1)


def solution(mesh):
    return jax.shard_map(
        local,
        mesh=mesh,
        in_specs=(
            P("inner", None),
            P(None, "inner"),
            P("storey", "inner"),
            P("storey", "inner"),
            P("storey", "inner"),
            P("inner", "storey", None),
            P("storey", None, None),
            P("storey", None),
        ),
        out_specs=P("inner", "storey", None),
        check_vma=False,
    )
```

```python
import jax
import jax.numpy as jnp
from jax import lax
from jax.experimental import pallas as pl
from jax.experimental.pallas import tpu as pltpu
from jax.sharding import PartitionSpec as P

MESH = pl.DeviceIdType.MESH
F32 = jnp.float32
BF16 = jnp.bfloat16

NX = 4
NW = 8
NZ = 8
CHUNKS = ((0, 384), (384, 384))
NK = len(CHUNKS)

NN = (((1,), (0,)), ((), ()))
NT = (((1,), (1,)), ((), ()))


def mm(a, b, dims):
    return lax.dot_general(a, b, dims, preferred_element_type=F32)


def kernel(
    load_ref, pivot_ref, transfer_ref, disp_ref, pairs_ref, weights_ref, analysis_hbm, synthesis_hbm,
    out_ref,
    A, S, E, acc, part, opp_out, opp_in, mid_out, mid_in, loc, gath, car, cgath,
    shift, group_in, zone_in, reply, coef, rate_group, rate_zone,
    tang, read_out, read_in, wread, adj,
    a_sem, s_sem, x_send, x_recv, k_send, k_recv, c_send, c_recv, r_send, r_recv, q_send, q_recv,
):
    storey = lax.axis_index("storey")
    x = lax.axis_index("inner")
    z = lax.div(storey, NW)
    w = lax.rem(storey, NW)
    rows, dofs = load_ref.shape
    cols = rows // 2
    half = cols // 2
    lane = cols // NW
    right, left, oppo = lax.rem(x + 1, NX), lax.rem(x + 3, NX), lax.rem(x + 2, NX)
    pending = []

    def xdev(i):
        return (storey, i)

    def wdev(i):
        return (z * NW + i, x)

    def zdev(i):
        return (i * NW + w, x)

    def remote(src, dst, ssem, rsem, dev):
        return pltpu.make_async_remote_copy(
            src_ref=src, dst_ref=dst, send_sem=ssem, recv_sem=rsem, device_id=dev, device_id_type=MESH
        )

    def send(src, dst, ssem, rsem, dev):
        c = remote(src, dst, ssem, rsem, dev)
        c.start()
        pending.append(c)

    def arrive(dst, ssem, rsem, dev):
        remote(dst, dst, ssem, rsem, dev).wait_recv()

    def lanes(k):
        return pl.ds(CHUNKS[k][0], CHUNKS[k][1])

    def block(t):
        return pl.ds(pl.multiple_of(t * dofs, 128), dofs)

    def modes(t, k):
        return pl.ds(pl.multiple_of(t * dofs + CHUNKS[k][0], 128), CHUNKS[k][1])

    targets = (oppo, right, left, x)
    a_copies = []
    for j, t in enumerate(targets):
        c = pltpu.make_async_copy(analysis_hbm.at[block(t), :], A.at[block(t), :], a_sem.at[j])
        c.start()
        a_copies.append(c)
    s_copy = pltpu.make_async_copy(synthesis_hbm, S, s_sem.at[0])
    s_copy.start()

    barrier = pltpu.get_barrier_semaphore()
    for d in range(1, NX):
        pl.semaphore_signal(barrier, inc=1, device_id=xdev(lax.rem(x + d, NX)), device_id_type=MESH)
    for d in range(1, NW):
        pl.semaphore_signal(barrier, inc=1, device_id=wdev(lax.rem(w + d, NW)), device_id_type=MESH)
    for d in range(1, NZ):
        pl.semaphore_signal(barrier, inc=1, device_id=zdev(lax.rem(z + d, NZ)), device_id_type=MESH)

    t0, t1 = transfer_ref[0:1, :], transfer_ref[1:2, :]
    p0, p1 = pivot_ref[0:1, :], pivot_ref[1:2, :]
    for n, row in enumerate((t0, t1, p0, p1, t0 * t1, t1 * p0, t0, t1)):
        coef[x, n : n + 1] = row

    def coefficients_first():
        for d in (2, 1, 3):
            i = lax.rem(x + d, NX)
            send(coef.at[x], coef.at[x], k_send.at[2, 0, i], k_recv.at[2, 0, x], xdev(i))

    def coefficients_second():
        for d in (1, 3, 2):
            i = lax.rem(x + d, NX)
            arrive(coef.at[i], k_send.at[2, 0, i], k_recv.at[2, 0, i], xdev(i))

    def rates_first():
        rate_group[w] = jnp.broadcast_to(t0 * t1, (8, dofs))
        for d in range(1, NW):
            i = lax.rem(w + d, NW)
            send(rate_group.at[w], rate_group.at[w], r_send.at[0, i], r_recv.at[0, w], wdev(i))

    def rates_second():
        for d in range(1, NW):
            i = lax.rem(w + d, NW)
            arrive(rate_group.at[i], r_send.at[0, i], r_recv.at[0, i], wdev(i))
        total = rate_group[0]
        for i in range(1, NW):
            total = total * rate_group[i]
        rate_zone[z] = total
        for d in range(1, NZ):
            i = lax.rem(z + d, NZ)
            send(rate_zone.at[z], rate_zone.at[z], r_send.at[1, i], r_recv.at[1, z], zdev(i))

    def rates_third():
        for d in range(1, NZ):
            i = lax.rem(z + d, NZ)
            arrive(rate_zone.at[i], r_send.at[1, i], r_recv.at[1, i], zdev(i))

    def build_incidence():
        sensors = pairs_ref.shape[2]
        for s in range(2):
            upper = pairs_ref[s, 0:1, :] - x * dofs
            lower = pairs_ref[s, 1:2, :] - x * dofs
            for b in range(0, dofs, 128):
                ids = lax.broadcasted_iota(jnp.int32, (128, sensors), 0) + b
                e = jnp.where(ids == upper, 1.0, 0.0) - jnp.where(ids == lower, 1.0, 0.0)
                E[s, b : b + 128] = e.astype(BF16)

    def project(v, j):
        t = targets[j]
        if v == 0:
            a_copies[j].wait()
            part[j] = mm(load_ref[...], A[block(t), :], NT)
        else:
            part[j] = mm(adj[...], S[:, block(t)], NN)

    def term(v, q, k, j, lo=0, n=cols):
        t = targets[j]
        low = part[j, lo : lo + n, lanes(k)]
        high = part[j, cols + lo : cols + lo + n, lanes(k)]
        if q == 1:
            return low if v == 0 else high
        if v == 0:
            return low * coef[t, 5:6, lanes(k)] + high * coef[t, 3:4, lanes(k)]
        return low + high * coef[t, 1:2, lanes(k)]

    def rs_opp(v, q, k):
        for n, dev in ((0, right), (1, left)):
            opp_out[v, q, n, :, lanes(k)] = term(v, q, k, 0, n * half, half).astype(BF16)
            send(
                opp_out.at[v, q, n, :, lanes(k)], opp_in.at[v, q, n, :, lanes(k)],
                x_send.at[v, q, k, n], x_recv.at[v, q, k, n], xdev(dev),
            )

    def rs_mid(v, q, k):
        for n, dev, back in ((0, right, left), (1, left, right)):
            arrive(opp_in.at[v, q, n, :, lanes(k)], x_send.at[v, q, k, n], x_recv.at[v, q, k, n], xdev(back))
            own, other = pl.ds(n * half, half), pl.ds((1 - n) * half, half)
            mine = term(v, q, k, 1 + n, n * half, half) + opp_in[v, q, n, :, lanes(k)].astype(F32)
            mid_out[v, q, n, own, lanes(k)] = mine.astype(BF16)
            mid_out[v, q, n, other, lanes(k)] = term(v, q, k, 1 + n, (1 - n) * half, half).astype(BF16)
            send(
                mid_out.at[v, q, n, :, lanes(k)], mid_in.at[v, q, n, :, lanes(k)],
                x_send.at[v, q, k, 2 + n], x_recv.at[v, q, k, 2 + n], xdev(dev),
            )

    def rs_end(v, q, k):
        for n, back in ((0, left), (1, right)):
            arrive(
                mid_in.at[v, q, n, :, lanes(k)], x_send.at[v, q, k, 2 + n], x_recv.at[v, q, k, 2 + n], xdev(back)
            )
        total = term(v, q, k, 3) + mid_in[v, q, 0, :, lanes(k)].astype(F32) + mid_in[v, q, 1, :, lanes(k)].astype(F32)
        if q == 0:
            out = total if v == 0 else total * coef[x, 0:1, lanes(k)]
            shift[v, :, :, lanes(k)] = out.astype(BF16).reshape(NW, lane, CHUNKS[k][1])
            for d in range(1, NW):
                i = lax.rem(w + d, NW)
                send(
                    shift.at[v, i, :, lanes(k)], group_in.at[v, w, :, lanes(k)],
                    c_send.at[v, k, 0, i], c_recv.at[v, k, 0, w], wdev(i),
                )
            group_in[v, w, :, lanes(k)] = shift[v, w, :, lanes(k)]
            if v == 1:
                total = total * coef[x, 2:3, lanes(k)]
        else:
            total = total * (coef[x, 2:3, lanes(k)] if v == 0 else coef[x, 3:4, lanes(k)])
        loc[v, q, :, lanes(k)] = total.astype(BF16)
        for n, dev in ((0, right), (1, left)):
            send(
                loc.at[v, q, :, lanes(k)], gath.at[v, q, n, :, lanes(k)],
                x_send.at[v, q, k, 4 + n], x_recv.at[v, q, k, 4 + n], xdev(dev),
            )

    def ag_second(v, q, k):
        for n, dev, back in ((0, right, left), (1, left, right)):
            arrive(gath.at[v, q, n, :, lanes(k)], x_send.at[v, q, k, 4 + n], x_recv.at[v, q, k, 4 + n], xdev(back))
            at = pl.ds(n * half, half)
            send(
                gath.at[v, q, n, at, lanes(k)], gath.at[v, q, 2, at, lanes(k)],
                x_send.at[v, q, k, 6 + n], x_recv.at[v, q, k, 6 + n], xdev(dev),
            )

    def ag_third(v, q, k):
        for n, back in ((0, left), (1, right)):
            at = pl.ds(n * half, half)
            arrive(gath.at[v, q, 2, at, lanes(k)], x_send.at[v, q, k, 6 + n], x_recv.at[v, q, k, 6 + n], xdev(back))

    def order(v, n):
        return range(n) if v == 0 else range(n - 1, -1, -1)

    def scan_second(v, k):
        for d in range(1, NW):
            i = lax.rem(w + d, NW)
            arrive(group_in.at[v, i, :, lanes(k)], c_send.at[v, k, 0, i], c_recv.at[v, k, 0, i], wdev(i))
        total = None
        for i in order(v, NW):
            new = group_in[v, i, :, lanes(k)].astype(F32)
            total = new if total is None else total * rate_group[i, 0:1, lanes(k)] + new
        zone_in[v, z, :, lanes(k)] = total.astype(BF16)
        for d in range(1, NZ):
            i = lax.rem(z + d, NZ)
            send(
                zone_in.at[v, z, :, lanes(k)], zone_in.at[v, z, :, lanes(k)],
                c_send.at[v, k, 1, i], c_recv.at[v, k, 1, z], zdev(i),
            )

    def scan_third(v, k):
        for d in range(1, NZ):
            i = lax.rem(z + d, NZ)
            arrive(zone_in.at[v, i, :, lanes(k)], c_send.at[v, k, 1, i], c_recv.at[v, k, 1, i], zdev(i))
        state = jnp.zeros((lane, CHUNKS[k][1]), F32)
        for i in order(v, NZ):
            ahead = (i < z) if v == 0 else (i > z)
            new = state * rate_zone[i, 0:1, lanes(k)] + zone_in[v, i, :, lanes(k)].astype(F32)
            state = jnp.where(ahead, new, state)
        for i in order(v, NW):
            reply[v, i, :, lanes(k)] = state.astype(BF16)
            state = state * rate_group[i, 0:1, lanes(k)] + group_in[v, i, :, lanes(k)].astype(F32)
        for d in range(1, NW):
            i = lax.rem(w + d, NW)
            send(
                reply.at[v, i, :, lanes(k)], car.at[v, w, :, lanes(k)],
                c_send.at[v, k, 2, i], c_recv.at[v, k, 2, w], wdev(i),
            )
        car[v, w, :, lanes(k)] = reply[v, w, :, lanes(k)]

    def carry_first(v, k):
        for d in range(1, NW):
            i = lax.rem(w + d, NW)
            arrive(car.at[v, i, :, lanes(k)], c_send.at[v, k, 2, i], c_recv.at[v, k, 2, i], wdev(i))
        for n, dev in ((2, oppo), (0, right), (1, left)):
            send(
                car.at[v, :, :, lanes(k)], cgath.at[v, n, :, :, lanes(k)],
                k_send.at[v, k, n], k_recv.at[v, k, n], xdev(dev),
            )

    def expand(v, k, n, first=False):
        t = (left, right, oppo, x)[n]
        width = CHUNKS[k][1]
        if n < 3:
            arrive(cgath.at[v, n, :, :, lanes(k)], k_send.at[v, k, n], k_recv.at[v, k, n], xdev(t))
            c = cgath[v, n, :, :, lanes(k)]
            lead, rest = gath[v, 0, n, :, lanes(k)], gath[v, 1, n, :, lanes(k)]
        else:
            c = car[v, :, :, lanes(k)]
            lead, rest = loc[v, 0, :, lanes(k)], loc[v, 1, :, lanes(k)]
        c = c.reshape(cols, width).astype(F32)
        lead, rest = lead.astype(F32), rest.astype(F32)
        if v == 0:
            low = rest + c * coef[t, 0:1, lanes(k)]
            high = lead + c * coef[t, 4:5, lanes(k)]
        else:
            low = lead + c * coef[t, 5:6, lanes(k)]
            high = rest + c * coef[t, 3:4, lanes(k)]
        val = jnp.concatenate([low.astype(BF16), high.astype(BF16)], axis=0)
        if v == 0:
            new = mm(val, S[:, modes(t, k)], NT)
        else:
            new = mm(val, A[modes(t, k), :], NN)
        acc[...] = new if first else acc[...] + new

    def sweep(v):
        if v == 0:
            project(0, 0)
            project(0, 1)
            pl.semaphore_wait(barrier, NX + NW + NZ - 3)
            coefficients_first()
            for k in range(NK):
                rs_opp(0, 1, k)
            rates_first()
            project(0, 2)
            project(0, 3)
            build_incidence()
            coefficients_second()
            for k in range(NK):
                rs_opp(0, 0, k)
            rs_mid(0, 1, 0)
            rates_second()
            for k in range(NK):
                rs_mid(0, 0, k)
            for k in range(1, NK):
                rs_mid(0, 1, k)
        else:
            project(1, 0)
            for q in range(2):
                for k in range(NK):
                    rs_opp(1, q, k)
            for j in range(1, 4):
                project(1, j)
            for q in range(2):
                for k in range(NK):
                    rs_mid(1, q, k)
        rs_end(v, 0, 0)
        rs_end(v, 0, 1)
        rs_end(v, 1, 0)
        scan_second(v, 0)
        rs_end(v, 1, 1)
        if v == 0:
            rates_third()
            s_copy.wait()
        scan_second(v, 1)
        ag_second(v, 0, 0)
        scan_third(v, 0)
        ag_second(v, 0, 1)
        scan_third(v, 1)
        ag_second(v, 1, 0)
        ag_second(v, 1, 1)
        carry_first(v, 0)
        carry_first(v, 1)
        expand(v, 0, 3, True)
        expand(v, 1, 3)
        for k in range(NK):
            expand(v, k, 0)
            expand(v, k, 1)
            for q in range(2):
                ag_third(v, q, k)
            expand(v, k, 2)

    sweep(0)

    quarter = rows // NX
    for s in range(2):
        tang[s] = acc[s * cols : (s + 1) * cols].astype(BF16)
        r = mm(tang[s], E[s], NN).astype(BF16)
        read_out[2 * s : 2 * s + 2] = r.reshape(2, quarter, r.shape[-1])
    for d in (2, 1, 3):
        i = lax.rem(x + d, NX)
        send(read_out.at[i], read_in.at[x], q_send.at[0, i], q_recv.at[0, x], xdev(i))
    read_in[x] = read_out[x]
    for d in (1, 3, 2):
        i = lax.rem(x + d, NX)
        arrive(read_in.at[i], q_send.at[0, i], q_recv.at[0, i], xdev(i))
    total = read_in[0].astype(F32)
    for i in range(1, NX):
        total = total + read_in[i].astype(F32)
    weight = weights_ref[pl.ds(lax.div(x, 2), 1), :]
    wread[x] = (total * weight).astype(BF16)
    for d in (2, 1, 3):
        i = lax.rem(x + d, NX)
        send(wread.at[x], wread.at[x], q_send.at[1, i], q_recv.at[1, x], xdev(i))
    for d in (1, 3, 2):
        i = lax.rem(x + d, NX)
        arrive(wread.at[i], q_send.at[1, i], q_recv.at[1, i], xdev(i))
    for s in range(2):
        r = wread[2 * s : 2 * s + 2].reshape(cols, wread.shape[-1])
        adj[s * cols : (s + 1) * cols] = mm(r, E[s], NT).astype(BF16)

    sweep(1)

    for s in range(2):
        at = slice(s * cols, (s + 1) * cols)
        out_ref[at] = -disp_ref[s : s + 1, :] * acc[at]
    for c in pending:
        c.wait_send()


def chain(load, pivot, transfer, disp, pairs, weights, analysis, synthesis):
    rows, dofs = load.shape
    modes = analysis.shape[0]
    cols = rows // 2
    lane = cols // NW
    sensors = pairs.shape[2]
    vm = pltpu.VMEM
    dma = pltpu.SemaphoreType.DMA
    scratch = [
        vm((modes, dofs), BF16),
        vm((dofs, modes), BF16),
        vm((2, dofs, sensors), BF16),
        vm((rows, dofs), F32),
        vm((4, rows, dofs), F32),
        vm((2, 2, 2, cols // 2, dofs), BF16),
        vm((2, 2, 2, cols // 2, dofs), BF16),
        vm((2, 2, 2, cols, dofs), BF16),
        vm((2, 2, 2, cols, dofs), BF16),
        vm((2, 2, cols, dofs), BF16),
        vm((2, 2, 3, cols, dofs), BF16),
        vm((2, NW, lane, dofs), BF16),
        vm((2, 3, NW, lane, dofs), BF16),
        vm((2, NW, lane, dofs), BF16),
        vm((2, NW, lane, dofs), BF16),
        vm((2, NZ, lane, dofs), BF16),
        vm((2, NW, lane, dofs), BF16),
        vm((NX, 8, dofs), F32),
        vm((NW, 8, dofs), F32),
        vm((NZ, 8, dofs), F32),
        vm((2, cols, dofs), BF16),
        vm((NX, rows // NX, sensors), BF16),
        vm((NX, rows // NX, sensors), BF16),
        vm((NX, rows // NX, sensors), BF16),
        vm((rows, dofs), BF16),
        dma((4,)), dma((1,)),
        dma((2, 2, NK, 8)), dma((2, 2, NK, 8)),
        dma((3, NK, 4)), dma((3, NK, 4)),
        dma((2, NK, 3, 8)), dma((2, NK, 3, 8)),
        dma((2, 8)), dma((2, 8)),
        dma((2, 4)), dma((2, 4)),
    ]
    in_vmem = pl.BlockSpec(memory_space=pltpu.VMEM)
    in_hbm = pl.BlockSpec(memory_space=pl.ANY)
    return pl.pallas_call(
        kernel,
        out_shape=jax.ShapeDtypeStruct((rows, dofs), F32),
        in_specs=[in_vmem] * 6 + [in_hbm] * 2,
        out_specs=in_vmem,
        scratch_shapes=scratch,
        compiler_params=pltpu.CompilerParams(
            collective_id=0, has_side_effects=True, vmem_limit_bytes=56 * 1024 * 1024
        ),
        cost_estimate=pl.CostEstimate(
            flops=8 * rows * modes * dofs, bytes_accessed=4 * modes * dofs, transcendentals=0
        ),
        name="chain",
    )(load, pivot, transfer, disp, pairs, weights, analysis, synthesis)


def local(synthesis, analysis, pivot, transfer, displacement, directions, sensor_pairs, sensor_weights):
    dofs, storeys, columns = directions.shape
    load = (-(displacement.T[:, :, None] * directions.astype(F32))).astype(BF16)
    load = load.transpose(1, 2, 0).reshape(storeys * columns, dofs)
    pairs = sensor_pairs.transpose(0, 2, 1)
    out = chain(load, pivot, transfer, displacement, pairs, sensor_weights, analysis, synthesis)
    return out.reshape(storeys, columns, dofs).transpose(2, 0, 1)


def solution(mesh):
    return jax.shard_map(
        local,
        mesh=mesh,
        in_specs=(
            P("inner", None),
            P(None, "inner"),
            P("storey", "inner"),
            P("storey", "inner"),
            P("storey", "inner"),
            P("inner", "storey", None),
            P("storey", None, None),
            P("storey", None),
        ),
        out_specs=P("inner", "storey", None),
        check_vma=False,
    )
```

```python
import jax
import jax.numpy as jnp
from jax import lax
from jax.experimental import pallas as pl
from jax.experimental.pallas import tpu as pltpu
from jax.sharding import PartitionSpec as P

MESH = pl.DeviceIdType.MESH
F32 = jnp.float32
BF16 = jnp.bfloat16

NX = 4
NW = 8
NZ = 8
NU = 2

NN = (((1,), (0,)), ((), ()))
NT = (((1,), (1,)), ((), ()))

ORDER = (
    "INC", "P002", "P001", "BAR", "COEF1", "RATE1", "P000", "OPP000", "OPP001", "P003", "P013", "P010", "OPP010",
    "OPP011", "P012", "P011", "COEF2", "RATE2", "MID000", "MID001", "MID010", "MID011", "END000", "RATE3", "END001",
    "END010", "END011", "SC200", "AG200", "SC201", "AG201", "SC300", "SC301", "CAR00", "EXP00", "CAR01", "EXP01",
    "EXQ00", "SEN10", "EXQ01", "SEN11", "SEN20", "SEN21", "ADJ0", "P100", "OPP100", "P102", "P103", "P101",
    "OPP101", "ADJ1", "P110", "OPP110", "MID100", "P111", "P112", "OPP111", "P113", "MID101", "MID110", "END100",
    "MID111", "END101", "SC210", "END110", "END111", "AG210", "SC211", "SC310", "AG211", "CAR10", "SC311", "EXP10",
    "CAR11", "EXP11", "EXQ10", "OUT0", "EXQ11", "OUT1",
)


def mm(a, b, dims):
    return lax.dot_general(a, b, dims, preferred_element_type=F32)


def kernel(
    load_ref, pivot_ref, transfer_ref, disp_ref, pairs_ref, weights_ref, analysis_hbm, synthesis_hbm,
    out_ref,
    A, S, E, acc, part, keep, opp_out, opp_in, mid_out, mid_in, early, early_in, late, late_in,
    shift, group_in, zone_in, reply, car, coef, rate_group, rate_zone,
    read_out, read_in, wread, adj,
    a_sem, s_sem, x_send, x_recv, k_send, k_recv, c_send, c_recv, r_send, r_recv, q_send, q_recv,
):
    storey = lax.axis_index("storey")
    x = lax.axis_index("inner")
    z = lax.div(storey, NW)
    w = lax.rem(storey, NW)
    rows, dofs = load_ref.shape
    cols = rows // 2
    hc = cols // NU
    half = hc // 2
    lane = 2 * hc // NW
    hm = dofs // 2
    right, left, oppo = lax.rem(x + 1, NX), lax.rem(x + 3, NX), lax.rem(x + 2, NX)
    pending = []

    def xdev(i):
        return (storey, i)

    def wdev(i):
        return (z * NW + i, x)

    def zdev(i):
        return (i * NW + w, x)

    def remote(src, dst, ssem, rsem, dev):
        return pltpu.make_async_remote_copy(
            src_ref=src, dst_ref=dst, send_sem=ssem, recv_sem=rsem, device_id=dev, device_id_type=MESH
        )

    def send(src, dst, ssem, rsem, dev):
        c = remote(src, dst, ssem, rsem, dev)
        c.start()
        pending.append(c)

    def arrive(dst, ssem, rsem, dev):
        remote(dst, dst, ssem, rsem, dev).wait_recv()

    def peers(me, n):
        return [lax.rem(me + d, n) for d in range(1, n)]

    xpeers, wpeers, zpeers = [oppo, right, left], peers(w, NW), peers(z, NZ)

    def block(t):
        return pl.ds(pl.multiple_of(t * dofs, 128), dofs)

    targets = (oppo, right, left, x)
    a_copies = {}
    for j in (0, 1, 2, 3):
        at = block(targets[j])
        c = pltpu.make_async_copy(analysis_hbm.at[at, :], A.at[at, :], a_sem.at[j])
        c.start()
        a_copies[j] = c
    s_copies = [pltpu.make_async_copy(synthesis_hbm, S, s_sem.at[0])]
    s_copies[0].start()

    barrier = pltpu.get_barrier_semaphore()
    for dev in [xdev(i) for i in xpeers] + [wdev(i) for i in wpeers] + [zdev(i) for i in zpeers]:
        pl.semaphore_signal(barrier, inc=1, device_id=dev, device_id_type=MESH)

    def entered():
        pl.semaphore_wait(barrier, NX + NW + NZ - 3)

    t0, t1 = transfer_ref[0:1, :], transfer_ref[1:2, :]
    p0, p1 = pivot_ref[0:1, :], pivot_ref[1:2, :]
    for n, row in enumerate((t0, t1, p0, p1, t0, t1, p0, p1)):
        coef[x, n : n + 1] = row

    def coefficients_first():
        for i in xpeers:
            send(coef.at[x], coef.at[x], k_send.at[2, 0, i], k_recv.at[2, 0, x], xdev(i))

    def coefficients_second():
        for i in xpeers:
            arrive(coef.at[i], k_send.at[2, 0, i], k_recv.at[2, 0, i], xdev(i))

    def rates_first():
        rate_group[w] = jnp.broadcast_to(t0 * t1, (8, dofs))
        for i in wpeers:
            send(rate_group.at[w], rate_group.at[w], r_send.at[0, i], r_recv.at[0, w], wdev(i))

    def rates_second():
        for i in wpeers:
            arrive(rate_group.at[i], r_send.at[0, i], r_recv.at[0, i], wdev(i))
        total = rate_group[0]
        for i in range(1, NW):
            total = total * rate_group[i]
        rate_zone[z] = total
        for i in zpeers:
            send(rate_zone.at[z], rate_zone.at[z], r_send.at[1, i], r_recv.at[1, z], zdev(i))

    def rates_third():
        for i in zpeers:
            arrive(rate_zone.at[i], r_send.at[1, i], r_recv.at[1, i], zdev(i))

    def build_incidence():
        sensors = pairs_ref.shape[2]
        for s in range(2):
            upper = pairs_ref[s, 0:1, :] - x * dofs
            lower = pairs_ref[s, 1:2, :] - x * dofs
            for b in range(0, dofs, 128):
                ids = lax.broadcasted_iota(jnp.int32, (128, sensors), 0) + b
                e = jnp.where(ids == upper, 1.0, 0.0) - jnp.where(ids == lower, 1.0, 0.0)
                E[s, b : b + 128] = e.astype(BF16)

    def project(v, k, j):
        t = targets[j]
        if v == 0:
            if j in a_copies:
                a_copies.pop(j).wait()
            val = jnp.concatenate([load_ref[s * cols + k * hc : s * cols + (k + 1) * hc, :] for s in range(2)], axis=0)
            part[k, j] = mm(val, A[block(t), :], NT)
        else:
            part[k, j] = mm(adj[k], S[:, block(t)], NN)

    def term(v, k, q, j, lo=0, n=hc):
        low = part[k, j, lo : lo + n]
        high = part[k, j, hc + lo : hc + lo + n]
        if v == 0:
            return high if q == 1 else low
        return high if q == 1 else low + high * coef[targets[j], 1:2, :]

    def rs_opp(v, k, q):
        for n, dev in ((0, right), (1, left)):
            opp_out[v, k, q, n] = term(v, k, q, 0, n * half, half).astype(BF16)
            send(
                opp_out.at[v, k, q, n], opp_in.at[v, k, q, n],
                x_send.at[v, k, q, n], x_recv.at[v, k, q, n], xdev(dev),
            )

    def rs_mid(v, k, q):
        for n, dev, back in ((0, right, left), (1, left, right)):
            arrive(opp_in.at[v, k, q, n], x_send.at[v, k, q, n], x_recv.at[v, k, q, n], xdev(back))
            own, other = n * half, (1 - n) * half
            mine = term(v, k, q, 1 + n, own, half) + opp_in[v, k, q, n].astype(F32)
            mid_out[v, k, q, n, own : own + half] = mine.astype(BF16)
            mid_out[v, k, q, n, other : other + half] = term(v, k, q, 1 + n, other, half).astype(BF16)
            send(
                mid_out.at[v, k, q, n], mid_in.at[v, k, q, n],
                x_send.at[v, k, q, 2 + n], x_recv.at[v, k, q, 2 + n], xdev(dev),
            )

    def rs_end(v, k, q):
        for n, back in ((0, left), (1, right)):
            arrive(mid_in.at[v, k, q, n], x_send.at[v, k, q, 2 + n], x_recv.at[v, k, q, 2 + n], xdev(back))
        total = term(v, k, q, 3) + mid_in[v, k, q, 0].astype(F32) + mid_in[v, k, q, 1].astype(F32)
        if v == 0:
            if q == 0:
                keep[k] = total * p0
            else:
                total = total * p1
                scan_first(v, k, keep[k] * t1 + total)
                early_first(v, k, total)
        else:
            if q == 0:
                keep[k] = total
                scan_first(v, k, total * t0)
            else:
                early_first(v, k, keep[k] - total * t1)
                keep[k] = total

    def early_first(v, k, val):
        early[v, k] = val.astype(BF16)
        for n, dev in ((0, right), (1, left)):
            send(early.at[v, k], early_in.at[v, k, n], x_send.at[v, k, n, 4], x_recv.at[v, k, n, 4], xdev(dev))

    def early_second(v, k):
        for n, dev, back in ((0, right, left), (1, left, right)):
            arrive(early_in.at[v, k, n], x_send.at[v, k, n, 4], x_recv.at[v, k, n, 4], xdev(back))
            at = pl.ds(n * half, half)
            send(
                early_in.at[v, k, n, at], early_in.at[v, k, 2, at],
                x_send.at[v, k, n, 5], x_recv.at[v, k, n, 5], xdev(dev),
            )

    def scan_first(v, k, val):
        val = val.astype(BF16)
        for h in range(2):
            shift[v, k, h * 4 : (h + 1) * 4] = val[:, h * hm : (h + 1) * hm].reshape(4, lane, hm)
        for i in wpeers:
            send(
                shift.at[v, k, i], group_in.at[v, k, w],
                c_send.at[v, k, 0, i], c_recv.at[v, k, 0, w], wdev(i),
            )
        group_in[v, k, w] = shift[v, k, w]

    def order(v, n):
        return range(n) if v == 0 else range(n - 1, -1, -1)

    def worker_lanes():
        return pl.ds(pl.multiple_of(lax.div(w, 4) * hm, 128), hm)

    def scan_second(v, k):
        for i in wpeers:
            arrive(group_in.at[v, k, i], c_send.at[v, k, 0, i], c_recv.at[v, k, 0, i], wdev(i))
        total = None
        for i in order(v, NW):
            new = group_in[v, k, i].astype(F32)
            total = new if total is None else total * rate_group[i, 0:1, worker_lanes()] + new
        zone_in[v, k, z] = total.astype(BF16)
        for i in zpeers:
            send(
                zone_in.at[v, k, z], zone_in.at[v, k, z],
                c_send.at[v, k, 1, i], c_recv.at[v, k, 1, z], zdev(i),
            )

    def scan_third(v, k):
        for i in zpeers:
            arrive(zone_in.at[v, k, i], c_send.at[v, k, 1, i], c_recv.at[v, k, 1, i], zdev(i))
        state = jnp.zeros((lane, hm), F32)
        for i in order(v, NZ):
            ahead = (i < z) if v == 0 else (i > z)
            new = state * rate_zone[i, 0:1, worker_lanes()] + zone_in[v, k, i].astype(F32)
            state = jnp.where(ahead, new, state)
        for i in order(v, NW):
            reply[v, k, i] = state.astype(BF16)
            state = state * rate_group[i, 0:1, worker_lanes()] + group_in[v, k, i].astype(F32)
        for i in wpeers:
            send(
                reply.at[v, k, i], car.at[v, k, w],
                c_send.at[v, k, 2, i], c_recv.at[v, k, 2, w], wdev(i),
            )
        car[v, k, w] = reply[v, k, w]

    def late_first(v, k):
        for i in wpeers:
            arrive(car.at[v, k, i], c_send.at[v, k, 2, i], c_recv.at[v, k, 2, i], wdev(i))
        for h in range(2):
            at = slice(h * hm, (h + 1) * hm)
            c = car[v, k, h * 4 : (h + 1) * 4].reshape(hc, hm).astype(F32)
            if v == 0:
                c = c * t0[:, at]
            late[v, k, :, at] = (keep[k, :, at] + c).astype(BF16)
        for n, dev in ((2, oppo), (0, right), (1, left)):
            send(late.at[v, k], late_in.at[v, k, n], k_send.at[v, k, n], k_recv.at[v, k, n], xdev(dev))

    def expand(v, k, n):
        t = (left, right, oppo, x)[n]
        if n == 3:
            last, first = late[v, k], early[v, k]
        else:
            if n == 2:
                for m, back in ((0, left), (1, right)):
                    at = pl.ds(m * half, half)
                    arrive(early_in.at[v, k, 2, at], x_send.at[v, k, m, 5], x_recv.at[v, k, m, 5], xdev(back))
            arrive(late_in.at[v, k, n], k_send.at[v, k, n], k_recv.at[v, k, n], xdev(t))
            last, first = late_in[v, k, n], early_in[v, k, n]
        grown = first.astype(F32) + last.astype(F32) * coef[t, 1:2, :]
        if v == 0:
            val = jnp.concatenate([last, grown.astype(BF16)], axis=0)
            new = mm(val, S[:, block(t)], NT)
        else:
            low = (grown * coef[t, 2:3, :]).astype(BF16)
            high = (last.astype(F32) * coef[t, 3:4, :]).astype(BF16)
            val = jnp.concatenate([low, high], axis=0)
            new = mm(val, A[block(t), :], NN)
        acc[k] = new if n == 3 else acc[k] + new

    def expand_own(v, k):
        if s_copies:
            s_copies.pop().wait()
        expand(v, k, 3)

    def expand_rest(v, k):
        for n in range(3):
            expand(v, k, n)

    quarter = 2 * hc // NX

    def sensors_first(k):
        for s in range(2):
            r = mm(acc[k, s * hc : (s + 1) * hc].astype(BF16), E[s], NN).astype(BF16)
            read_out[k, 2 * s : 2 * s + 2] = r.reshape(2, quarter, r.shape[-1])
        for i in xpeers:
            send(read_out.at[k, i], read_in.at[k, x], q_send.at[k, 0, i], q_recv.at[k, 0, x], xdev(i))
        read_in[k, x] = read_out[k, x]

    def sensors_second(k):
        for i in xpeers:
            arrive(read_in.at[k, i], q_send.at[k, 0, i], q_recv.at[k, 0, i], xdev(i))
        total = read_in[k, 0].astype(F32)
        for i in range(1, NX):
            total = total + read_in[k, i].astype(F32)
        weight = weights_ref[pl.ds(lax.div(x, 2), 1), :]
        wread[k, x] = (total * weight).astype(BF16)
        for i in xpeers:
            send(wread.at[k, x], wread.at[k, x], q_send.at[k, 1, i], q_recv.at[k, 1, x], xdev(i))

    def sensors_third(k):
        for i in xpeers:
            arrive(wread.at[k, i], q_send.at[k, 1, i], q_recv.at[k, 1, i], xdev(i))
        for s in range(2):
            r = wread[k, 2 * s : 2 * s + 2].reshape(hc, wread.shape[-1])
            adj[k, s * hc : (s + 1) * hc] = mm(r, E[s], NT).astype(BF16)

    def finish(k):
        for s in range(2):
            at = s * cols + k * hc
            out_ref[at : at + hc] = -disp_ref[s : s + 1, :] * acc[k, s * hc : (s + 1) * hc]

    steps = {
        "INC": build_incidence, "BAR": entered, "COEF1": coefficients_first, "COEF2": coefficients_second,
        "RATE1": rates_first, "RATE2": rates_second, "RATE3": rates_third,
        "P": project, "OPP": rs_opp, "MID": rs_mid, "END": rs_end, "AG2": early_second,
        "SC2": scan_second, "SC3": scan_third, "CAR": late_first, "EXP": expand_own, "EXQ": expand_rest,
        "SEN1": sensors_first, "SEN2": sensors_second, "ADJ": sensors_third, "OUT": finish,
    }
    for name in ORDER:
        if name in steps:
            steps[name]()
            continue
        stem = name[:1] if name[0] == "P" else name[:4] if name[:3] == "SEN" else name[:3]
        steps[stem](*(int(d) for d in name[len(stem) :]))
    for c in pending:
        c.wait_send()


def chain(load, pivot, transfer, disp, pairs, weights, analysis, synthesis):
    rows, dofs = load.shape
    modes = analysis.shape[0]
    cols = rows // 2
    sensors = pairs.shape[2]
    vm = pltpu.VMEM
    dma = pltpu.SemaphoreType.DMA
    hc = cols // NU
    hm = dofs // 2
    lane = 2 * hc // NW
    scratch = [
        vm((modes, dofs), BF16),
        vm((dofs, modes), BF16),
        vm((2, dofs, sensors), BF16),
        vm((NU, 2 * hc, dofs), F32),
        vm((NU, 4, 2 * hc, dofs), F32),
        vm((NU, hc, dofs), F32),
        vm((2, NU, 2, 2, hc // 2, dofs), BF16),
        vm((2, NU, 2, 2, hc // 2, dofs), BF16),
        vm((2, NU, 2, 2, hc, dofs), BF16),
        vm((2, NU, 2, 2, hc, dofs), BF16),
        vm((2, NU, hc, dofs), BF16),
        vm((2, NU, 3, hc, dofs), BF16),
        vm((2, NU, hc, dofs), BF16),
        vm((2, NU, 3, hc, dofs), BF16),
        vm((2, NU, NW, lane, hm), BF16),
        vm((2, NU, NW, lane, hm), BF16),
        vm((2, NU, NZ, lane, hm), BF16),
        vm((2, NU, NW, lane, hm), BF16),
        vm((2, NU, NW, lane, hm), BF16),
        vm((NX, 8, dofs), F32),
        vm((NW, 8, dofs), F32),
        vm((NZ, 8, dofs), F32),
        vm((NU, NX, 2 * hc // NX, sensors), BF16),
        vm((NU, NX, 2 * hc // NX, sensors), BF16),
        vm((NU, NX, 2 * hc // NX, sensors), BF16),
        vm((NU, 2 * hc, dofs), BF16),
        dma((4,)), dma((1,)),
        dma((2, NU, 2, 6)), dma((2, NU, 2, 6)),
        dma((3, NU, 4)), dma((3, NU, 4)),
        dma((2, NU, 3, 8)), dma((2, NU, 3, 8)),
        dma((2, 8)), dma((2, 8)),
        dma((NU, 2, 4)), dma((NU, 2, 4)),
    ]
    in_vmem = pl.BlockSpec(memory_space=pltpu.VMEM)
    in_hbm = pl.BlockSpec(memory_space=pl.ANY)
    return pl.pallas_call(
        kernel,
        out_shape=jax.ShapeDtypeStruct((rows, dofs), F32),
        in_specs=[in_vmem] * 6 + [in_hbm] * 2,
        out_specs=in_vmem,
        scratch_shapes=scratch,
        compiler_params=pltpu.CompilerParams(
            collective_id=0, has_side_effects=True, vmem_limit_bytes=56 * 1024 * 1024
        ),
        cost_estimate=pl.CostEstimate(
            flops=8 * rows * modes * dofs, bytes_accessed=4 * modes * dofs, transcendentals=0
        ),
        name="chain",
    )(load, pivot, transfer, disp, pairs, weights, analysis, synthesis)


def local(synthesis, analysis, pivot, transfer, displacement, directions, sensor_pairs, sensor_weights):
    dofs, storeys, columns = directions.shape
    load = (-(displacement.T[:, :, None] * directions.astype(F32))).astype(BF16)
    load = load.transpose(1, 2, 0).reshape(storeys * columns, dofs)
    pairs = sensor_pairs.transpose(0, 2, 1)
    out = chain(load, pivot, transfer, displacement, pairs, sensor_weights, analysis, synthesis)
    return out.reshape(storeys, columns, dofs).transpose(2, 0, 1)


def solution(mesh):
    return jax.shard_map(
        local,
        mesh=mesh,
        in_specs=(
            P("inner", None),
            P(None, "inner"),
            P("storey", "inner"),
            P("storey", "inner"),
            P("storey", "inner"),
            P("inner", "storey", None),
            P("storey", None, None),
            P("storey", None),
        ),
        out_specs=P("inner", "storey", None),
        check_vma=False,
    )
```

```python
import jax
import jax.numpy as jnp
from jax import lax
from jax.experimental import pallas as pl
from jax.experimental.pallas import tpu as pltpu
from jax.sharding import PartitionSpec as P

MESH = pl.DeviceIdType.MESH
F32 = jnp.float32
BF16 = jnp.bfloat16

NX = 4
NW = 8
NZ = 8
NU = 2

NN = (((1,), (0,)), ((), ()))
NT = (((1,), (1,)), ((), ()))

ORDER = (
    "P000", "BAR", "OPP000", "COEF1", "OPP001", "P013", "P003", "RATE1", "P001", "P002", "P011", "P010", "OPP010",
    "OPP011", "INC", "P012", "MID000", "COEF2", "RATE2", "MID001", "MID010", "MID011", "END000", "RATE3", "END001",
    "END010", "END011", "SC200", "AG200", "SC201", "AG201", "SC300", "SC301", "CAR00", "EXP00", "CAR01", "EXP01",
    "EXQ00", "SEN10", "EXQ01", "SEN11", "SEN20", "SEN21", "ADJ0", "P101", "P100", "OPP100", "OPP101", "P102",
    "P103", "ADJ1", "P110", "OPP110", "P113", "OPP111", "P111", "P112", "MID100", "MID101", "MID110", "MID111",
    "END100", "END101", "END110", "SC210", "END111", "AG210", "SC211", "SC310", "AG211", "SC311", "CAR10", "EXP10",
    "CAR11", "EXP11", "EXQ10", "OUT0", "EXQ11", "OUT1",
)


def mm(a, b, dims):
    return lax.dot_general(a, b, dims, preferred_element_type=F32)


def kernel(
    directions_hbm, pivot_hbm, transfer_hbm, disp_hbm, pairs_hbm, weights_hbm, analysis_hbm, synthesis_hbm,
    out_ref,
    directions_ref, pivot_ref, transfer_ref, disp_ref, pairs_ref, weights_ref, load_ref,
    A, S, E, acc, part, keep, opp_out, opp_in, mid_out, mid_in, early, early_in, late, late_in,
    shift, group_in, zone_in, reply, car, coef, rate_group, rate_zone,
    read_out, read_in, wread, adj,
    in_sem, a_sem, s_sem, x_send, x_recv, k_send, k_recv, c_send, c_recv, r_send, r_recv, q_send, q_recv,
):
    storey = lax.axis_index("storey")
    x = lax.axis_index("inner")
    z = lax.div(storey, NW)
    w = lax.rem(storey, NW)
    dofs, _, cols = directions_ref.shape
    rows = 2 * cols
    hc = cols // NU
    half = hc // 2
    lane = 2 * hc // NW
    hm = dofs // 2
    right, left, oppo = lax.rem(x + 1, NX), lax.rem(x + 3, NX), lax.rem(x + 2, NX)
    pending = []

    def xdev(i):
        return (storey, i)

    def wdev(i):
        return (z * NW + i, x)

    def zdev(i):
        return (i * NW + w, x)

    def remote(src, dst, ssem, rsem, dev):
        return pltpu.make_async_remote_copy(
            src_ref=src, dst_ref=dst, send_sem=ssem, recv_sem=rsem, device_id=dev, device_id_type=MESH
        )

    def send(src, dst, ssem, rsem, dev):
        c = remote(src, dst, ssem, rsem, dev)
        c.start()
        pending.append(c)

    def arrive(dst, ssem, rsem, dev):
        remote(dst, dst, ssem, rsem, dev).wait_recv()

    def peers(me, n):
        return [lax.rem(me + d, n) for d in range(1, n)]

    xpeers, wpeers, zpeers = [oppo, right, left], peers(w, NW), peers(z, NZ)

    def block(t):
        return pl.ds(pl.multiple_of(t * dofs, 128), dofs)

    barrier = pltpu.get_barrier_semaphore()
    for dev in [zdev(i) for i in zpeers] + [wdev(i) for i in wpeers] + [xdev(i) for i in xpeers]:
        pl.semaphore_signal(barrier, inc=1, device_id=dev, device_id_type=MESH)

    def entered():
        pl.semaphore_wait(barrier, NX + NW + NZ - 3)

    def fetch(src, dst, sem):
        c = pltpu.make_async_copy(src, dst, sem)
        c.start()
        return c

    targets = (oppo, right, left, x)
    small = [fetch(directions_hbm, directions_ref, in_sem.at[0]), fetch(disp_hbm, disp_ref, in_sem.at[1])]
    a_copies = {0: fetch(analysis_hbm.at[block(targets[0]), :], A.at[block(targets[0]), :], a_sem.at[0])}
    others = ((pivot_hbm, pivot_ref), (transfer_hbm, transfer_ref), (pairs_hbm, pairs_ref), (weights_hbm, weights_ref))
    more = [fetch(src, dst, in_sem.at[2 + n]) for n, (src, dst) in enumerate(others)]
    for j in (1, 2, 3):
        a_copies[j] = fetch(analysis_hbm.at[block(targets[j]), :], A.at[block(targets[j]), :], a_sem.at[j])
    s_copies = [fetch(synthesis_hbm, S, s_sem.at[0])]

    for c in small:
        c.wait()
    for b in range(0, dofs, 128):
        both = directions_ref[b : b + 128].astype(F32)
        for s in range(2):
            turned = jnp.transpose(both[:, s, :], (1, 0))
            load_ref[s * cols : (s + 1) * cols, b : b + 128] = (-disp_ref[s : s + 1, b : b + 128] * turned).astype(BF16)
    for c in more:
        c.wait()

    t0, t1 = transfer_ref[0:1, :], transfer_ref[1:2, :]
    p0, p1 = pivot_ref[0:1, :], pivot_ref[1:2, :]
    for n, row in enumerate((t0, t1, p0, p1, t0, t1, p0, p1)):
        coef[x, n : n + 1] = row

    def coefficients_first():
        for i in xpeers:
            send(coef.at[x], coef.at[x], k_send.at[2, 0, i], k_recv.at[2, 0, x], xdev(i))

    def coefficients_second():
        for i in xpeers:
            arrive(coef.at[i], k_send.at[2, 0, i], k_recv.at[2, 0, i], xdev(i))

    def rates_first():
        rate_group[w] = jnp.broadcast_to(t0 * t1, (8, dofs))
        for i in wpeers:
            send(rate_group.at[w], rate_group.at[w], r_send.at[0, i], r_recv.at[0, w], wdev(i))

    def rates_second():
        for i in wpeers:
            arrive(rate_group.at[i], r_send.at[0, i], r_recv.at[0, i], wdev(i))
        total = rate_group[0]
        for i in range(1, NW):
            total = total * rate_group[i]
        rate_zone[z] = total
        for i in zpeers:
            send(rate_zone.at[z], rate_zone.at[z], r_send.at[1, i], r_recv.at[1, z], zdev(i))

    def rates_third():
        for i in zpeers:
            arrive(rate_zone.at[i], r_send.at[1, i], r_recv.at[1, i], zdev(i))

    def build_incidence():
        sensors = pairs_ref.shape[2]
        for s in range(2):
            upper = pairs_ref[s, 0:1, :] - x * dofs
            lower = pairs_ref[s, 1:2, :] - x * dofs
            for b in range(0, dofs, 128):
                ids = lax.broadcasted_iota(jnp.int32, (128, sensors), 0) + b
                e = jnp.where(ids == upper, 1.0, 0.0) - jnp.where(ids == lower, 1.0, 0.0)
                E[s, b : b + 128] = e.astype(BF16)

    def project(v, k, j):
        t = targets[j]
        if v == 0:
            if j in a_copies:
                a_copies.pop(j).wait()
            val = jnp.concatenate([load_ref[s * cols + k * hc : s * cols + (k + 1) * hc, :] for s in range(2)], axis=0)
            part[k, j] = mm(val, A[block(t), :], NT)
        else:
            part[k, j] = mm(adj[k], S[:, block(t)], NN)

    def term(v, k, q, j, lo=0, n=hc):
        low = part[k, j, lo : lo + n]
        high = part[k, j, hc + lo : hc + lo + n]
        if v == 0:
            return high if q == 1 else low
        return high if q == 1 else low + high * coef[targets[j], 1:2, :]

    def rs_opp(v, k, q):
        for n, dev in ((0, right), (1, left)):
            opp_out[v, k, q, n] = term(v, k, q, 0, n * half, half).astype(BF16)
            send(
                opp_out.at[v, k, q, n], opp_in.at[v, k, q, n],
                x_send.at[v, k, q, n], x_recv.at[v, k, q, n], xdev(dev),
            )

    def rs_mid(v, k, q):
        for n, dev, back in ((0, right, left), (1, left, right)):
            arrive(opp_in.at[v, k, q, n], x_send.at[v, k, q, n], x_recv.at[v, k, q, n], xdev(back))
            own, other = n * half, (1 - n) * half
            mine = term(v, k, q, 1 + n, own, half) + opp_in[v, k, q, n].astype(F32)
            mid_out[v, k, q, n, own : own + half] = mine.astype(BF16)
            mid_out[v, k, q, n, other : other + half] = term(v, k, q, 1 + n, other, half).astype(BF16)
            send(
                mid_out.at[v, k, q, n], mid_in.at[v, k, q, n],
                x_send.at[v, k, q, 2 + n], x_recv.at[v, k, q, 2 + n], xdev(dev),
            )

    def rs_end(v, k, q):
        for n, back in ((0, left), (1, right)):
            arrive(mid_in.at[v, k, q, n], x_send.at[v, k, q, 2 + n], x_recv.at[v, k, q, 2 + n], xdev(back))
        total = term(v, k, q, 3) + mid_in[v, k, q, 0].astype(F32) + mid_in[v, k, q, 1].astype(F32)
        if v == 0:
            if q == 0:
                keep[k] = total * p0
            else:
                total = total * p1
                scan_first(v, k, keep[k] * t1 + total)
                early_first(v, k, total)
        else:
            if q == 0:
                keep[k] = total
                scan_first(v, k, total * t0)
            else:
                early_first(v, k, keep[k] - total * t1)
                keep[k] = total

    def early_first(v, k, val):
        early[v, k] = val.astype(BF16)
        for n, dev in ((0, right), (1, left)):
            send(early.at[v, k], early_in.at[v, k, n], x_send.at[v, k, n, 4], x_recv.at[v, k, n, 4], xdev(dev))

    def early_second(v, k):
        for n, dev, back in ((0, right, left), (1, left, right)):
            arrive(early_in.at[v, k, n], x_send.at[v, k, n, 4], x_recv.at[v, k, n, 4], xdev(back))
            at = pl.ds(n * half, half)
            send(
                early_in.at[v, k, n, at], early_in.at[v, k, 2, at],
                x_send.at[v, k, n, 5], x_recv.at[v, k, n, 5], xdev(dev),
            )

    def scan_first(v, k, val):
        val = val.astype(BF16)
        for h in range(2):
            shift[v, k, h * 4 : (h + 1) * 4] = val[:, h * hm : (h + 1) * hm].reshape(4, lane, hm)
        for i in wpeers:
            send(
                shift.at[v, k, i], group_in.at[v, k, w],
                c_send.at[v, k, 0, i], c_recv.at[v, k, 0, w], wdev(i),
            )
        group_in[v, k, w] = shift[v, k, w]

    def order(v, n):
        return range(n) if v == 0 else range(n - 1, -1, -1)

    def worker_lanes():
        return pl.ds(pl.multiple_of(lax.div(w, 4) * hm, 128), hm)

    def scan_second(v, k):
        for i in wpeers:
            arrive(group_in.at[v, k, i], c_send.at[v, k, 0, i], c_recv.at[v, k, 0, i], wdev(i))
        total = None
        for i in order(v, NW):
            new = group_in[v, k, i].astype(F32)
            total = new if total is None else total * rate_group[i, 0:1, worker_lanes()] + new
        zone_in[v, k, z] = total.astype(BF16)
        for i in zpeers:
            send(
                zone_in.at[v, k, z], zone_in.at[v, k, z],
                c_send.at[v, k, 1, i], c_recv.at[v, k, 1, z], zdev(i),
            )

    def scan_third(v, k):
        for i in zpeers:
            arrive(zone_in.at[v, k, i], c_send.at[v, k, 1, i], c_recv.at[v, k, 1, i], zdev(i))
        state = jnp.zeros((lane, hm), F32)
        for i in order(v, NZ):
            ahead = (i < z) if v == 0 else (i > z)
            new = state * rate_zone[i, 0:1, worker_lanes()] + zone_in[v, k, i].astype(F32)
            state = jnp.where(ahead, new, state)
        for i in order(v, NW):
            reply[v, k, i] = state.astype(BF16)
            state = state * rate_group[i, 0:1, worker_lanes()] + group_in[v, k, i].astype(F32)
        for i in wpeers:
            send(
                reply.at[v, k, i], car.at[v, k, w],
                c_send.at[v, k, 2, i], c_recv.at[v, k, 2, w], wdev(i),
            )
        car[v, k, w] = reply[v, k, w]

    def late_first(v, k):
        for i in wpeers:
            arrive(car.at[v, k, i], c_send.at[v, k, 2, i], c_recv.at[v, k, 2, i], wdev(i))
        for h in range(2):
            at = slice(h * hm, (h + 1) * hm)
            c = car[v, k, h * 4 : (h + 1) * 4].reshape(hc, hm).astype(F32)
            if v == 0:
                c = c * t0[:, at]
            late[v, k, :, at] = (keep[k, :, at] + c).astype(BF16)
        for n, dev in ((2, oppo), (0, right), (1, left)):
            send(late.at[v, k], late_in.at[v, k, n], k_send.at[v, k, n], k_recv.at[v, k, n], xdev(dev))

    def expand(v, k, n):
        t = (left, right, oppo, x)[n]
        if n == 3:
            last, first = late[v, k], early[v, k]
        else:
            if n == 2:
                for m, back in ((0, left), (1, right)):
                    at = pl.ds(m * half, half)
                    arrive(early_in.at[v, k, 2, at], x_send.at[v, k, m, 5], x_recv.at[v, k, m, 5], xdev(back))
            arrive(late_in.at[v, k, n], k_send.at[v, k, n], k_recv.at[v, k, n], xdev(t))
            last, first = late_in[v, k, n], early_in[v, k, n]
        grown = first.astype(F32) + last.astype(F32) * coef[t, 1:2, :]
        if v == 0:
            val = jnp.concatenate([last, grown.astype(BF16)], axis=0)
            new = mm(val, S[:, block(t)], NT)
        else:
            low = (grown * coef[t, 2:3, :]).astype(BF16)
            high = (last.astype(F32) * coef[t, 3:4, :]).astype(BF16)
            val = jnp.concatenate([low, high], axis=0)
            new = mm(val, A[block(t), :], NN)
        acc[k] = new if n == 3 else acc[k] + new

    def expand_own(v, k):
        if s_copies:
            s_copies.pop().wait()
        expand(v, k, 3)

    def expand_rest(v, k):
        for n in range(3):
            expand(v, k, n)

    quarter = 2 * hc // NX

    def sensors_first(k):
        for s in range(2):
            r = mm(acc[k, s * hc : (s + 1) * hc].astype(BF16), E[s], NN).astype(BF16)
            read_out[k, 2 * s : 2 * s + 2] = r.reshape(2, quarter, r.shape[-1])
        for i in xpeers:
            send(read_out.at[k, i], read_in.at[k, x], q_send.at[k, 0, i], q_recv.at[k, 0, x], xdev(i))
        read_in[k, x] = read_out[k, x]

    def sensors_second(k):
        for i in xpeers:
            arrive(read_in.at[k, i], q_send.at[k, 0, i], q_recv.at[k, 0, i], xdev(i))
        total = read_in[k, 0].astype(F32)
        for i in range(1, NX):
            total = total + read_in[k, i].astype(F32)
        weight = weights_ref[pl.ds(lax.div(x, 2), 1), :]
        wread[k, x] = (total * weight).astype(BF16)
        for i in xpeers:
            send(wread.at[k, x], wread.at[k, x], q_send.at[k, 1, i], q_recv.at[k, 1, x], xdev(i))

    def sensors_third(k):
        for i in xpeers:
            arrive(wread.at[k, i], q_send.at[k, 1, i], q_recv.at[k, 1, i], xdev(i))
        for s in range(2):
            r = wread[k, 2 * s : 2 * s + 2].reshape(hc, wread.shape[-1])
            adj[k, s * hc : (s + 1) * hc] = mm(r, E[s], NT).astype(BF16)

    def finish(k):
        for s in range(2):
            at = s * cols + k * hc
            out_ref[at : at + hc] = -disp_ref[s : s + 1, :] * acc[k, s * hc : (s + 1) * hc]

    steps = {
        "INC": build_incidence, "BAR": entered, "COEF1": coefficients_first, "COEF2": coefficients_second,
        "RATE1": rates_first, "RATE2": rates_second, "RATE3": rates_third,
        "P": project, "OPP": rs_opp, "MID": rs_mid, "END": rs_end, "AG2": early_second,
        "SC2": scan_second, "SC3": scan_third, "CAR": late_first, "EXP": expand_own, "EXQ": expand_rest,
        "SEN1": sensors_first, "SEN2": sensors_second, "ADJ": sensors_third, "OUT": finish,
    }
    for name in ORDER:
        if name in steps:
            steps[name]()
            continue
        stem = name[:1] if name[0] == "P" else name[:4] if name[:3] == "SEN" else name[:3]
        steps[stem](*(int(d) for d in name[len(stem) :]))
    for c in pending:
        c.wait_send()


def chain(directions, pivot, transfer, disp, pairs, weights, analysis, synthesis):
    dofs, _, cols = directions.shape
    rows = 2 * cols
    modes = analysis.shape[0]
    sensors = pairs.shape[2]
    vm = pltpu.VMEM
    dma = pltpu.SemaphoreType.DMA
    hc = cols // NU
    hm = dofs // 2
    lane = 2 * hc // NW
    small = (directions, pivot, transfer, disp, pairs, weights)
    scratch = [vm(a.shape, a.dtype) for a in small] + [
        vm((rows, dofs), BF16),
        vm((modes, dofs), BF16),
        vm((dofs, modes), BF16),
        vm((2, dofs, sensors), BF16),
        vm((NU, 2 * hc, dofs), F32),
        vm((NU, 4, 2 * hc, dofs), F32),
        vm((NU, hc, dofs), F32),
        vm((2, NU, 2, 2, hc // 2, dofs), BF16),
        vm((2, NU, 2, 2, hc // 2, dofs), BF16),
        vm((2, NU, 2, 2, hc, dofs), BF16),
        vm((2, NU, 2, 2, hc, dofs), BF16),
        vm((2, NU, hc, dofs), BF16),
        vm((2, NU, 3, hc, dofs), BF16),
        vm((2, NU, hc, dofs), BF16),
        vm((2, NU, 3, hc, dofs), BF16),
        vm((2, NU, NW, lane, hm), BF16),
        vm((2, NU, NW, lane, hm), BF16),
        vm((2, NU, NZ, lane, hm), BF16),
        vm((2, NU, NW, lane, hm), BF16),
        vm((2, NU, NW, lane, hm), BF16),
        vm((NX, 8, dofs), F32),
        vm((NW, 8, dofs), F32),
        vm((NZ, 8, dofs), F32),
        vm((NU, NX, 2 * hc // NX, sensors), BF16),
        vm((NU, NX, 2 * hc // NX, sensors), BF16),
        vm((NU, NX, 2 * hc // NX, sensors), BF16),
        vm((NU, 2 * hc, dofs), BF16),
        dma((6,)), dma((4,)), dma((1,)),
        dma((2, NU, 2, 6)), dma((2, NU, 2, 6)),
        dma((3, NU, 4)), dma((3, NU, 4)),
        dma((2, NU, 3, 8)), dma((2, NU, 3, 8)),
        dma((2, 8)), dma((2, 8)),
        dma((NU, 2, 4)), dma((NU, 2, 4)),
    ]
    in_vmem = pl.BlockSpec(memory_space=pltpu.VMEM)
    in_hbm = pl.BlockSpec(memory_space=pl.ANY)
    return pl.pallas_call(
        kernel,
        out_shape=jax.ShapeDtypeStruct((rows, dofs), F32),
        in_specs=[in_hbm] * 8,
        out_specs=in_vmem,
        scratch_shapes=scratch,
        compiler_params=pltpu.CompilerParams(
            collective_id=0, has_side_effects=True, vmem_limit_bytes=56 * 1024 * 1024
        ),
        cost_estimate=pl.CostEstimate(
            flops=8 * rows * modes * dofs, bytes_accessed=4 * modes * dofs, transcendentals=0
        ),
        name="chain",
    )(directions, pivot, transfer, disp, pairs, weights, analysis, synthesis)


def local(synthesis, analysis, pivot, transfer, displacement, directions, sensor_pairs, sensor_weights):
    dofs, storeys, columns = directions.shape
    pairs = sensor_pairs.transpose(0, 2, 1)
    out = chain(directions, pivot, transfer, displacement, pairs, sensor_weights, analysis, synthesis)
    return out.reshape(storeys, columns, dofs).transpose(2, 0, 1)


def solution(mesh):
    return jax.shard_map(
        local,
        mesh=mesh,
        in_specs=(
            P("inner", None),
            P(None, "inner"),
            P("storey", "inner"),
            P("storey", "inner"),
            P("storey", "inner"),
            P("inner", "storey", None),
            P("storey", None, None),
            P("storey", None),
        ),
        out_specs=P("inner", "storey", None),
        check_vma=False,
    )
```

```python
import jax
import jax.numpy as jnp
from jax import lax
from jax.experimental import pallas as pl
from jax.experimental.pallas import tpu as pltpu
from jax.sharding import PartitionSpec as P

MESH = pl.DeviceIdType.MESH
F32 = jnp.float32
BF16 = jnp.bfloat16

NX = 4
NW = 8
NZ = 8
NU = 2

NN = (((1,), (0,)), ((), ()))
NT = (((1,), (1,)), ((), ()))

ORDER = (
    "BAR", "COEF1", "P000", "OPP000", "P012", "Z0", "P003", "OPP001", "P010", "OPP011", "OPP010", "P001", "P002",
    "RATE1", "Z1", "P013", "P011", "INC", "COEF2", "Z2", "MID000", "MID001", "Z3", "RATE2", "MID011", "MID010",
    "END000", "END001", "RATE3", "END010", "SC200", "END011", "AG200", "SC201", "AG201", "CAR00", "CAR01", "EXP00",
    "EXQ001", "EXQ002", "EXQ000", "SEN10", "EXP01", "EXQ011", "EXQ010", "EXQ012", "SEN11", "SEN20", "SEN21", "ADJ0",
    "P100", "OPP100", "P101", "P102", "P103", "OPP101", "ADJ1", "P110", "OPP110", "P113", "P112", "MID100",
    "OPP111", "P111", "MID101", "MID110", "END100", "MID111", "END101", "SC210", "END110", "END111", "AG210",
    "SC211", "CAR10", "AG211", "CAR11", "EXP10", "EXQ102", "EXQ100", "EXQ101", "OUT0", "EXP11", "EXQ111", "EXQ112",
    "EXQ110", "OUT1",
)


def mm(a, b, dims):
    return lax.dot_general(a, b, dims, preferred_element_type=F32)


def kernel(
    directions_hbm, pivot_hbm, transfer_hbm, disp_hbm, pairs_hbm, weights_hbm, analysis_hbm, synthesis_hbm,
    out_ref,
    directions_ref, pivot_ref, transfer_ref, disp_ref, pairs_ref, weights_ref, load_ref,
    A, S, E, acc, part, keep, opp_out, opp_in, mid_out, mid_in, early, early_in, late_in,
    shift, group_in, base, base_in, zone_in, reply, coef, rate_group, rate_zone,
    read_out, read_in, wread, adj,
    z_sem, in_sem, a_sem, s_sem, x_send, x_recv, k_send, k_recv, l_send, l_recv, a_recv,
    c_send, c_recv, r_send, r_recv, q_send, q_recv,
):
    storey = lax.axis_index("storey")
    x = lax.axis_index("inner")
    z = lax.div(storey, NW)
    w = lax.rem(storey, NW)
    dofs, _, cols = directions_ref.shape
    rows = 2 * cols
    hc = cols // NU
    half = hc // 2
    lane = 2 * hc // NW
    hm = dofs // 2
    right, left, oppo = lax.rem(x + 1, NX), lax.rem(x + 3, NX), lax.rem(x + 2, NX)
    pending = []

    def xdev(i):
        return (storey, i)

    def wdev(i):
        return (z * NW + i, x)

    def zdev(i):
        return (i * NW + w, x)

    def remote(src, dst, ssem, rsem, dev):
        return pltpu.make_async_remote_copy(
            src_ref=src, dst_ref=dst, send_sem=ssem, recv_sem=rsem, device_id=dev, device_id_type=MESH
        )

    def send(src, dst, ssem, rsem, dev):
        c = remote(src, dst, ssem, rsem, dev)
        c.start()
        pending.append(c)

    def arrive(dst, ssem, rsem, dev):
        remote(dst, dst, ssem, rsem, dev).wait_recv()

    def peers(me, n):
        return [lax.rem(me + d, n) for d in range(1, n)]

    xpeers, wpeers, zpeers = [oppo, right, left], peers(w, NW), peers(z, NZ)

    def block(t):
        return pl.ds(pl.multiple_of(t * dofs, 128), dofs)

    barrier = pltpu.get_barrier_semaphore()
    znext = (lax.rem(z + 1, NZ), lax.rem(z + NZ - 1, NZ))
    for dev in [xdev(i) for i in xpeers] + [wdev(i) for i in wpeers] + [zdev(i) for i in znext]:
        pl.semaphore_signal(barrier, inc=1, device_id=dev, device_id_type=MESH)

    def entered():
        pl.semaphore_wait(barrier, NX + NW)

    def along(r):
        for n in range(2):
            if r > 0:
                pl.semaphore_wait(z_sem.at[r - 1, n], 1)
            if r < 3:
                pl.semaphore_signal(z_sem.at[r, n], inc=1, device_id=zdev(znext[n]), device_id_type=MESH)

    def fetch(src, dst, sem):
        c = pltpu.make_async_copy(src, dst, sem)
        c.start()
        return c

    targets = (oppo, right, left, x)
    small = [fetch(directions_hbm, directions_ref, in_sem.at[0]), fetch(disp_hbm, disp_ref, in_sem.at[1])]
    a_copies = {0: fetch(analysis_hbm.at[block(targets[0]), :], A.at[block(targets[0]), :], a_sem.at[0])}
    others = ((pivot_hbm, pivot_ref), (transfer_hbm, transfer_ref), (pairs_hbm, pairs_ref), (weights_hbm, weights_ref))
    more = [fetch(src, dst, in_sem.at[2 + n]) for n, (src, dst) in enumerate(others)]
    for j in (1, 2, 3):
        a_copies[j] = fetch(analysis_hbm.at[block(targets[j]), :], A.at[block(targets[j]), :], a_sem.at[j])
    s_copies = [fetch(synthesis_hbm, S, s_sem.at[0])]

    for c in small:
        c.wait()
    for b in range(0, dofs, 128):
        both = directions_ref[b : b + 128].astype(F32)
        for s in range(2):
            turned = jnp.transpose(both[:, s, :], (1, 0))
            load_ref[s * cols : (s + 1) * cols, b : b + 128] = (-disp_ref[s : s + 1, b : b + 128] * turned).astype(BF16)
    for c in more:
        c.wait()

    t0, t1 = transfer_ref[0:1, :], transfer_ref[1:2, :]
    p0, p1 = pivot_ref[0:1, :], pivot_ref[1:2, :]
    for n, row in enumerate((t0, t1, p0, p1, t0, t1, p0, p1)):
        coef[x, n : n + 1] = row

    def coefficients_first():
        for i in xpeers:
            send(coef.at[x], coef.at[x], k_send.at[i], k_recv.at[x], xdev(i))

    def coefficients_second():
        for i in xpeers:
            arrive(coef.at[i], k_send.at[i], k_recv.at[i], xdev(i))

    def rates_first():
        rate_group[w, 0:1] = t0 * t1
        rate_group[w, 1:2] = t0
        rate_group[w, 2:8] = jnp.broadcast_to(t0, (6, dofs))
        for i in wpeers:
            send(rate_group.at[w], rate_group.at[w], r_send.at[0, i], r_recv.at[0, w], wdev(i))

    def rates_second():
        for i in wpeers:
            arrive(rate_group.at[i], r_send.at[0, i], r_recv.at[0, i], wdev(i))
        total = rate_group[0]
        for i in range(1, NW):
            total = total * rate_group[i]
        rate_zone[z] = total
        for i in zpeers:
            send(rate_zone.at[z], rate_zone.at[z], r_send.at[1, i], r_recv.at[1, z], zdev(i))

    def rates_third():
        for i in zpeers:
            arrive(rate_zone.at[i], r_send.at[1, i], r_recv.at[1, i], zdev(i))

    def build_incidence():
        sensors = pairs_ref.shape[2]
        for s in range(2):
            upper = pairs_ref[s, 0:1, :] - x * dofs
            lower = pairs_ref[s, 1:2, :] - x * dofs
            for b in range(0, dofs, 128):
                ids = lax.broadcasted_iota(jnp.int32, (128, sensors), 0) + b
                e = jnp.where(ids == upper, 1.0, 0.0) - jnp.where(ids == lower, 1.0, 0.0)
                E[s, b : b + 128] = e.astype(BF16)

    def project(v, k, j):
        t = targets[j]
        if v == 0:
            if j in a_copies:
                a_copies.pop(j).wait()
            val = jnp.concatenate([load_ref[s * cols + k * hc : s * cols + (k + 1) * hc, :] for s in range(2)], axis=0)
            part[k, j] = mm(val, A[block(t), :], NT)
        else:
            part[k, j] = mm(adj[k], S[:, block(t)], NN)

    def term(v, k, q, j, lo=0, n=hc):
        low = part[k, j, lo : lo + n]
        high = part[k, j, hc + lo : hc + lo + n]
        if v == 0:
            return high if q == 1 else low
        return high if q == 1 else low + high * coef[targets[j], 1:2, :]

    def rs_opp(v, k, q):
        for n, dev in ((0, right), (1, left)):
            opp_out[v, k, q, n] = term(v, k, q, 0, n * half, half).astype(BF16)
            send(
                opp_out.at[v, k, q, n], opp_in.at[v, k, q, n],
                x_send.at[v, k, q, n], x_recv.at[v, k, q, n], xdev(dev),
            )

    def rs_mid(v, k, q):
        for n, dev, back in ((0, right, left), (1, left, right)):
            arrive(opp_in.at[v, k, q, n], x_send.at[v, k, q, n], x_recv.at[v, k, q, n], xdev(back))
            own, other = n * half, (1 - n) * half
            mine = term(v, k, q, 1 + n, own, half) + opp_in[v, k, q, n].astype(F32)
            mid_out[v, k, q, n, own : own + half] = mine.astype(BF16)
            mid_out[v, k, q, n, other : other + half] = term(v, k, q, 1 + n, other, half).astype(BF16)
            send(
                mid_out.at[v, k, q, n], mid_in.at[v, k, q, n],
                x_send.at[v, k, q, 2 + n], x_recv.at[v, k, q, 2 + n], xdev(dev),
            )

    def rs_end(v, k, q):
        for n, back in ((0, left), (1, right)):
            arrive(mid_in.at[v, k, q, n], x_send.at[v, k, q, 2 + n], x_recv.at[v, k, q, 2 + n], xdev(back))
        total = term(v, k, q, 3) + mid_in[v, k, q, 0].astype(F32) + mid_in[v, k, q, 1].astype(F32)
        if v == 0:
            if q == 0:
                keep[k] = total * p0
            else:
                total = total * p1
                scan_first(v, k, keep[k] * t1 + total)
                to_workers(v, k, 2, base, base_in, keep[k])
                early_first(v, k, total)
        else:
            if q == 0:
                keep[k] = total
                scan_first(v, k, total * t0)
            else:
                to_workers(v, k, 2, base, base_in, total)
                early_first(v, k, keep[k] - total * t1)

    def early_first(v, k, val):
        early[v, k] = val.astype(BF16)
        for n, dev in ((0, right), (1, left)):
            send(early.at[v, k], early_in.at[v, k, n], x_send.at[v, k, n, 4], x_recv.at[v, k, n, 4], xdev(dev))

    def early_second(v, k):
        for n, dev, back in ((0, right, left), (1, left, right)):
            arrive(early_in.at[v, k, n], x_send.at[v, k, n, 4], x_recv.at[v, k, n, 4], xdev(back))
            at = pl.ds(n * half, half)
            send(
                early_in.at[v, k, n, at], early_in.at[v, k, 2, at],
                x_send.at[v, k, n, 5], x_recv.at[v, k, n, 5], xdev(dev),
            )

    def to_workers(v, k, stage, out, into, val):
        val = val.astype(BF16)
        for h in range(2):
            out[v, k, h * 4 : (h + 1) * 4] = val[:, h * hm : (h + 1) * hm].reshape(4, lane, hm)
        for i in wpeers:
            send(
                out.at[v, k, i], into.at[v, k, w],
                c_send.at[v, k, stage, i], c_recv.at[v, k, stage, w], wdev(i),
            )
        into[v, k, w] = out[v, k, w]

    def scan_first(v, k, val):
        to_workers(v, k, 0, shift, group_in, val)

    def order(v, n):
        return range(n) if v == 0 else range(n - 1, -1, -1)

    def worker_lanes():
        return pl.ds(pl.multiple_of(lax.div(w, 4) * hm, 128), hm)

    def scan_second(v, k):
        for i in wpeers:
            arrive(group_in.at[v, k, i], c_send.at[v, k, 0, i], c_recv.at[v, k, 0, i], wdev(i))
        total = None
        for i in order(v, NW):
            new = group_in[v, k, i].astype(F32)
            total = new if total is None else total * rate_group[i, 0:1, worker_lanes()] + new
        zone_in[v, k, z] = total.astype(BF16)
        for i in zpeers:
            send(
                zone_in.at[v, k, z], zone_in.at[v, k, z],
                c_send.at[v, k, 1, i], c_recv.at[v, k, 1, z], zdev(i),
            )

    def scan_third(v, k):
        for i in zpeers:
            arrive(zone_in.at[v, k, i], c_send.at[v, k, 1, i], c_recv.at[v, k, 1, i], zdev(i))
        for i in wpeers:
            arrive(base_in.at[v, k, i], c_send.at[v, k, 2, i], c_recv.at[v, k, 2, i], wdev(i))
        state = jnp.zeros((lane, hm), F32)
        for i in order(v, NZ):
            ahead = (i < z) if v == 0 else (i > z)
            new = state * rate_zone[i, 0:1, worker_lanes()] + zone_in[v, k, i].astype(F32)
            state = jnp.where(ahead, new, state)
        for i in order(v, NW):
            grown = state * rate_group[i, 1:2, worker_lanes()] if v == 0 else state
            reply[v, k, i] = (base_in[v, k, i].astype(F32) + grown).astype(BF16)
            state = state * rate_group[i, 0:1, worker_lanes()] + group_in[v, k, i].astype(F32)
        for i in wpeers:
            send(
                reply.at[v, k, i], late_in.at[v, k, x, w],
                l_send.at[v, k, 0, i], l_recv.at[v, k, 0, w], wdev(i),
            )
        for d, t in enumerate(xpeers):
            for i in [w] + wpeers:
                send(
                    reply.at[v, k, i], late_in.at[v, k, x, w],
                    l_send.at[v, k, 1 + d, i], a_recv.at[v, k, x], (z * NW + i, t),
                )
        late_in[v, k, x, w] = reply[v, k, w]

    def expand(v, k, n):
        t = (left, right, oppo, x)[n]
        if n == 3:
            for i in wpeers:
                arrive(late_in.at[v, k, x, i], l_send.at[v, k, 0, i], l_recv.at[v, k, 0, i], wdev(i))
            first = early[v, k]
        else:
            if n == 2:
                for m, back in ((0, left), (1, right)):
                    at = pl.ds(m * half, half)
                    arrive(early_in.at[v, k, 2, at], x_send.at[v, k, m, 5], x_recv.at[v, k, m, 5], xdev(back))
            arrive(late_in.at[v, k, t], l_send.at[v, k, 1, 0], a_recv.at[v, k, t], xdev(t))
            first = early_in[v, k, n]
        last = jnp.concatenate([late_in[v, k, t, h * 4 : (h + 1) * 4].reshape(hc, hm) for h in range(2)], axis=1)
        grown = first.astype(F32) + last.astype(F32) * coef[t, 1:2, :]
        if v == 0:
            val = jnp.concatenate([last, grown.astype(BF16)], axis=0)
            new = mm(val, S[:, block(t)], NT)
        else:
            low = (grown * coef[t, 2:3, :]).astype(BF16)
            high = (last.astype(F32) * coef[t, 3:4, :]).astype(BF16)
            val = jnp.concatenate([low, high], axis=0)
            new = mm(val, A[block(t), :], NN)
        acc[k] = new if n == 3 else acc[k] + new

    def expand_own(v, k):
        if s_copies:
            s_copies.pop().wait()
        expand(v, k, 3)

    quarter = 2 * hc // NX

    def sensors_first(k):
        for s in range(2):
            r = mm(acc[k, s * hc : (s + 1) * hc].astype(BF16), E[s], NN).astype(BF16)
            read_out[k, 2 * s : 2 * s + 2] = r.reshape(2, quarter, r.shape[-1])
        for i in xpeers:
            send(read_out.at[k, i], read_in.at[k, x], q_send.at[k, 0, i], q_recv.at[k, 0, x], xdev(i))
        read_in[k, x] = read_out[k, x]

    def sensors_second(k):
        for i in xpeers:
            arrive(read_in.at[k, i], q_send.at[k, 0, i], q_recv.at[k, 0, i], xdev(i))
        total = read_in[k, 0].astype(F32)
        for i in range(1, NX):
            total = total + read_in[k, i].astype(F32)
        weight = weights_ref[pl.ds(lax.div(x, 2), 1), :]
        wread[k, x] = (total * weight).astype(BF16)
        for i in xpeers:
            send(wread.at[k, x], wread.at[k, x], q_send.at[k, 1, i], q_recv.at[k, 1, x], xdev(i))

    def sensors_third(k):
        for i in xpeers:
            arrive(wread.at[k, i], q_send.at[k, 1, i], q_recv.at[k, 1, i], xdev(i))
        for s in range(2):
            r = wread[k, 2 * s : 2 * s + 2].reshape(hc, wread.shape[-1])
            adj[k, s * hc : (s + 1) * hc] = mm(r, E[s], NT).astype(BF16)

    def finish(k):
        for s in range(2):
            at = s * cols + k * hc
            out_ref[at : at + hc] = -disp_ref[s : s + 1, :] * acc[k, s * hc : (s + 1) * hc]

    steps = {
        "INC": build_incidence, "BAR": entered, "Z": along, "COEF1": coefficients_first, "COEF2": coefficients_second,
        "RATE1": rates_first, "RATE2": rates_second, "RATE3": rates_third,
        "P": project, "OPP": rs_opp, "MID": rs_mid, "END": rs_end, "AG2": early_second,
        "SC2": scan_second, "CAR": scan_third, "EXP": expand_own, "EXQ": expand,
        "SEN1": sensors_first, "SEN2": sensors_second, "ADJ": sensors_third, "OUT": finish,
    }
    for name in ORDER:
        if name in steps:
            steps[name]()
            continue
        stem = name[:1] if name[0] in "PZ" else name[:4] if name[:3] == "SEN" else name[:3]
        steps[stem](*(int(d) for d in name[len(stem) :]))
    for c in pending:
        c.wait_send()


def chain(directions, pivot, transfer, disp, pairs, weights, analysis, synthesis):
    dofs, _, cols = directions.shape
    rows = 2 * cols
    modes = analysis.shape[0]
    sensors = pairs.shape[2]
    vm = pltpu.VMEM
    dma = pltpu.SemaphoreType.DMA
    hc = cols // NU
    hm = dofs // 2
    lane = 2 * hc // NW
    small = (directions, pivot, transfer, disp, pairs, weights)
    scratch = [vm(a.shape, a.dtype) for a in small] + [
        vm((rows, dofs), BF16),
        vm((modes, dofs), BF16),
        vm((dofs, modes), BF16),
        vm((2, dofs, sensors), BF16),
        vm((NU, 2 * hc, dofs), F32),
        vm((NU, 4, 2 * hc, dofs), F32),
        vm((NU, hc, dofs), F32),
        vm((2, NU, 2, 2, hc // 2, dofs), BF16),
        vm((2, NU, 2, 2, hc // 2, dofs), BF16),
        vm((2, NU, 2, 2, hc, dofs), BF16),
        vm((2, NU, 2, 2, hc, dofs), BF16),
        vm((2, NU, hc, dofs), BF16),
        vm((2, NU, 3, hc, dofs), BF16),
        vm((2, NU, NX, NW, lane, hm), BF16),
        vm((2, NU, NW, lane, hm), BF16),
        vm((2, NU, NW, lane, hm), BF16),
        vm((2, NU, NW, lane, hm), BF16),
        vm((2, NU, NW, lane, hm), BF16),
        vm((2, NU, NZ, lane, hm), BF16),
        vm((2, NU, NW, lane, hm), BF16),
        vm((NX, 8, dofs), F32),
        vm((NW, 8, dofs), F32),
        vm((NZ, 8, dofs), F32),
        vm((NU, NX, 2 * hc // NX, sensors), BF16),
        vm((NU, NX, 2 * hc // NX, sensors), BF16),
        vm((NU, NX, 2 * hc // NX, sensors), BF16),
        vm((NU, 2 * hc, dofs), BF16),
        pltpu.SemaphoreType.REGULAR((3, 2)),
        dma((6,)), dma((4,)), dma((1,)),
        dma((2, NU, 2, 6)), dma((2, NU, 2, 6)),
        dma((NX,)), dma((NX,)),
        dma((2, NU, NX, NW)), dma((2, NU, 1, NW)), dma((2, NU, NX)),
        dma((2, NU, 3, 8)), dma((2, NU, 3, 8)),
        dma((2, 8)), dma((2, 8)),
        dma((NU, 2, 4)), dma((NU, 2, 4)),
    ]
    in_vmem = pl.BlockSpec(memory_space=pltpu.VMEM)
    in_hbm = pl.BlockSpec(memory_space=pl.ANY)
    return pl.pallas_call(
        kernel,
        out_shape=jax.ShapeDtypeStruct((rows, dofs), F32),
        in_specs=[in_hbm] * 8,
        out_specs=in_vmem,
        scratch_shapes=scratch,
        compiler_params=pltpu.CompilerParams(
            collective_id=0, has_side_effects=True, vmem_limit_bytes=56 * 1024 * 1024
        ),
        cost_estimate=pl.CostEstimate(
            flops=8 * rows * modes * dofs, bytes_accessed=4 * modes * dofs, transcendentals=0
        ),
        name="chain",
    )(directions, pivot, transfer, disp, pairs, weights, analysis, synthesis)


def local(synthesis, analysis, pivot, transfer, displacement, directions, sensor_pairs, sensor_weights):
    dofs, storeys, columns = directions.shape
    pairs = sensor_pairs.transpose(0, 2, 1)
    out = chain(directions, pivot, transfer, displacement, pairs, sensor_weights, analysis, synthesis)
    return out.reshape(storeys, columns, dofs).transpose(2, 0, 1)


def solution(mesh):
    return jax.shard_map(
        local,
        mesh=mesh,
        in_specs=(
            P("inner", None),
            P(None, "inner"),
            P("storey", "inner"),
            P("storey", "inner"),
            P("storey", "inner"),
            P("inner", "storey", None),
            P("storey", None, None),
            P("storey", None),
        ),
        out_specs=P("inner", "storey", None),
        check_vma=False,
    )
```

```python
import jax
import jax.numpy as jnp
from jax import lax
from jax.experimental import pallas as pl
from jax.experimental.pallas import tpu as pltpu
from jax.sharding import PartitionSpec as P

MESH = pl.DeviceIdType.MESH
F32 = jnp.float32
BF16 = jnp.bfloat16

NX = 4
NW = 8
NZ = 8
NU = 2

NN = (((1,), (0,)), ((), ()))
NT = (((1,), (1,)), ((), ()))

ORDER = (
    "BAR", "COEF1", "P000", "OPP000", "P012", "Z0", "P003", "OPP001", "P010", "OPP011", "OPP010", "P001", "P002",
    "RATE1", "Z1", "P013", "P011", "INC", "COEF2", "Z2", "MID000", "MID001", "Z3", "RATE2", "MID011", "MID010",
    "END000", "END001", "RATE3", "END010", "SC200", "END011", "AG200", "SC201", "AG201", "CAR00", "CAR01", "FL80",
    "EXP00", "EXQ001", "EXQ002", "EXQ000", "SEN10", "EXP01", "EXQ011", "EXQ010", "EXQ012", "SEN11", "SEN20",
    "SEN21", "FL12", "ADJ0", "P100", "OPP100", "P101", "P102", "P103", "OPP101", "ADJ1", "P110", "OPP110", "P113",
    "P112", "MID100", "OPP111", "P111", "MID101", "MID110", "END100", "MID111", "FL24", "END101", "SC210", "END110",
    "END111", "AG210", "FL40", "SC211", "CAR10", "AG211", "CAR11", "FL66", "EXP10", "EXQ102", "EXQ100", "EXQ101",
    "OUT0", "FL31", "EXP11", "EXQ111", "EXQ112", "EXQ110", "OUT1",
)


def mm(a, b, dims):
    return lax.dot_general(a, b, dims, preferred_element_type=F32)


def kernel(
    directions_hbm, pivot_hbm, transfer_hbm, disp_hbm, pairs_hbm, weights_hbm, analysis_hbm, synthesis_hbm,
    out_ref,
    directions_ref, pivot_ref, transfer_ref, disp_ref, pairs_ref, weights_ref, load_ref,
    A, S, E, acc, part, keep, opp_out, opp_in, mid_out, mid_in, early, early_in, late_in,
    shift, group_in, base, base_in, zone_in, reply, coef, rate_group, rate_zone,
    read_out, read_in, wread, adj,
    z_sem, in_sem, a_sem, s_sem, x_send, x_recv, k_send, k_recv, l_send, l_recv, a_recv,
    c_send, c_recv, r_send, r_recv, q_send, q_recv,
):
    storey = lax.axis_index("storey")
    x = lax.axis_index("inner")
    z = lax.div(storey, NW)
    w = lax.rem(storey, NW)
    dofs, _, cols = directions_ref.shape
    rows = 2 * cols
    hc = cols // NU
    half = hc // 2
    lane = 2 * hc // NW
    hm = dofs // 2
    right, left, oppo = lax.rem(x + 1, NX), lax.rem(x + 3, NX), lax.rem(x + 2, NX)
    pending = []

    def xdev(i):
        return (storey, i)

    def wdev(i):
        return (z * NW + i, x)

    def zdev(i):
        return (i * NW + w, x)

    def remote(src, dst, ssem, rsem, dev):
        return pltpu.make_async_remote_copy(
            src_ref=src, dst_ref=dst, send_sem=ssem, recv_sem=rsem, device_id=dev, device_id_type=MESH
        )

    def send(src, dst, ssem, rsem, dev):
        c = remote(src, dst, ssem, rsem, dev)
        c.start()
        pending.append(c)

    def flush(keep):
        while len(pending) > keep:
            pending.pop(0).wait_send()

    def arrive(dst, ssem, rsem, dev):
        remote(dst, dst, ssem, rsem, dev).wait_recv()

    def peers(me, n):
        far_first = sorted(range(1, n), key=lambda d: -min(d, n - d))
        return [lax.rem(me + d, n) for d in far_first]

    xpeers, wpeers, zpeers = [oppo, right, left], peers(w, NW), peers(z, NZ)

    def block(t):
        return pl.ds(pl.multiple_of(t * dofs, 128), dofs)

    barrier = pltpu.get_barrier_semaphore()
    znext = (lax.rem(z + 1, NZ), lax.rem(z + NZ - 1, NZ))
    for dev in [xdev(i) for i in xpeers] + [wdev(i) for i in wpeers] + [zdev(i) for i in znext]:
        pl.semaphore_signal(barrier, inc=1, device_id=dev, device_id_type=MESH)

    def entered():
        pl.semaphore_wait(barrier, NX + NW)

    def along(r):
        for n in range(2):
            if r > 0:
                pl.semaphore_wait(z_sem.at[r - 1, n], 1)
            if r < 3:
                pl.semaphore_signal(z_sem.at[r, n], inc=1, device_id=zdev(znext[n]), device_id_type=MESH)

    def fetch(src, dst, sem):
        c = pltpu.make_async_copy(src, dst, sem)
        c.start()
        return c

    targets = (oppo, right, left, x)
    small = [fetch(directions_hbm, directions_ref, in_sem.at[0]), fetch(disp_hbm, disp_ref, in_sem.at[1])]
    a_copies = {0: fetch(analysis_hbm.at[block(targets[0]), :], A.at[block(targets[0]), :], a_sem.at[0])}
    others = ((pivot_hbm, pivot_ref), (transfer_hbm, transfer_ref), (pairs_hbm, pairs_ref), (weights_hbm, weights_ref))
    more = [fetch(src, dst, in_sem.at[2 + n]) for n, (src, dst) in enumerate(others)]
    for j in (1, 2, 3):
        a_copies[j] = fetch(analysis_hbm.at[block(targets[j]), :], A.at[block(targets[j]), :], a_sem.at[j])
    s_copies = [fetch(synthesis_hbm, S, s_sem.at[0])]

    for c in small:
        c.wait()
    for b in range(0, dofs, 128):
        both = directions_ref[b : b + 128].astype(F32)
        for s in range(2):
            turned = jnp.transpose(both[:, s, :], (1, 0))
            load_ref[s * cols : (s + 1) * cols, b : b + 128] = (-disp_ref[s : s + 1, b : b + 128] * turned).astype(BF16)
    for c in more:
        c.wait()

    t0, t1 = transfer_ref[0:1, :], transfer_ref[1:2, :]
    p0, p1 = pivot_ref[0:1, :], pivot_ref[1:2, :]
    for n, row in enumerate((t0, t1, p0, p1, t0, t1, p0, p1)):
        coef[x, n : n + 1] = row

    def coefficients_first():
        for i in xpeers:
            send(coef.at[x], coef.at[x], k_send.at[i], k_recv.at[x], xdev(i))

    def coefficients_second():
        for i in xpeers:
            arrive(coef.at[i], k_send.at[i], k_recv.at[i], xdev(i))

    def rates_first():
        rate_group[w, 0:1] = t0 * t1
        rate_group[w, 1:2] = t0
        rate_group[w, 2:8] = jnp.broadcast_to(t0, (6, dofs))
        for i in wpeers:
            send(rate_group.at[w], rate_group.at[w], r_send.at[0, i], r_recv.at[0, w], wdev(i))

    def rates_second():
        for i in wpeers:
            arrive(rate_group.at[i], r_send.at[0, i], r_recv.at[0, i], wdev(i))
        total = rate_group[0]
        for i in range(1, NW):
            total = total * rate_group[i]
        rate_zone[z] = total
        for i in zpeers:
            send(rate_zone.at[z], rate_zone.at[z], r_send.at[1, i], r_recv.at[1, z], zdev(i))

    def rates_third():
        for i in zpeers:
            arrive(rate_zone.at[i], r_send.at[1, i], r_recv.at[1, i], zdev(i))

    def build_incidence():
        sensors = pairs_ref.shape[2]
        for s in range(2):
            upper = pairs_ref[s, 0:1, :] - x * dofs
            lower = pairs_ref[s, 1:2, :] - x * dofs
            for b in range(0, dofs, 128):
                ids = lax.broadcasted_iota(jnp.int32, (128, sensors), 0) + b
                e = jnp.where(ids == upper, 1.0, 0.0) - jnp.where(ids == lower, 1.0, 0.0)
                E[s, b : b + 128] = e.astype(BF16)

    def project(v, k, j):
        t = targets[j]
        if v == 0:
            if j in a_copies:
                a_copies.pop(j).wait()
            val = jnp.concatenate([load_ref[s * cols + k * hc : s * cols + (k + 1) * hc, :] for s in range(2)], axis=0)
            part[k, j] = mm(val, A[block(t), :], NT)
        else:
            part[k, j] = mm(adj[k], S[:, block(t)], NN)

    def term(v, k, q, j, lo=0, n=hc):
        low = part[k, j, lo : lo + n]
        high = part[k, j, hc + lo : hc + lo + n]
        if v == 0:
            return high if q == 1 else low
        return high if q == 1 else low + high * coef[targets[j], 1:2, :]

    def rs_opp(v, k, q):
        for n, dev in ((0, right), (1, left)):
            opp_out[v, k, q, n] = term(v, k, q, 0, n * half, half).astype(BF16)
            send(
                opp_out.at[v, k, q, n], opp_in.at[v, k, q, n],
                x_send.at[v, k, q, n], x_recv.at[v, k, q, n], xdev(dev),
            )

    def rs_mid(v, k, q):
        for n, dev, back in ((0, right, left), (1, left, right)):
            arrive(opp_in.at[v, k, q, n], x_send.at[v, k, q, n], x_recv.at[v, k, q, n], xdev(back))
            own, other = n * half, (1 - n) * half
            mine = term(v, k, q, 1 + n, own, half) + opp_in[v, k, q, n].astype(F32)
            mid_out[v, k, q, n, own : own + half] = mine.astype(BF16)
            mid_out[v, k, q, n, other : other + half] = term(v, k, q, 1 + n, other, half).astype(BF16)
            send(
                mid_out.at[v, k, q, n], mid_in.at[v, k, q, n],
                x_send.at[v, k, q, 2 + n], x_recv.at[v, k, q, 2 + n], xdev(dev),
            )

    def rs_end(v, k, q):
        for n, back in ((0, left), (1, right)):
            arrive(mid_in.at[v, k, q, n], x_send.at[v, k, q, 2 + n], x_recv.at[v, k, q, 2 + n], xdev(back))
        total = term(v, k, q, 3) + mid_in[v, k, q, 0].astype(F32) + mid_in[v, k, q, 1].astype(F32)
        if v == 0:
            if q == 0:
                keep[k] = total * p0
            else:
                total = total * p1
                scan_first(v, k, keep[k] * t1 + total)
                early_first(v, k, total)
                to_workers(v, k, 2, base, base_in, keep[k])
        else:
            if q == 0:
                keep[k] = total
                scan_first(v, k, total * t0)
            else:
                early_first(v, k, keep[k] - total * t1)
                to_workers(v, k, 2, base, base_in, total)

    def early_first(v, k, val):
        early[v, k] = val.astype(BF16)
        for n, dev in ((0, right), (1, left)):
            send(early.at[v, k], early_in.at[v, k, n], x_send.at[v, k, n, 4], x_recv.at[v, k, n, 4], xdev(dev))

    def early_second(v, k):
        for n, dev, back in ((0, right, left), (1, left, right)):
            arrive(early_in.at[v, k, n], x_send.at[v, k, n, 4], x_recv.at[v, k, n, 4], xdev(back))
            at = pl.ds(n * half, half)
            send(
                early_in.at[v, k, n, at], early_in.at[v, k, 2, at],
                x_send.at[v, k, n, 5], x_recv.at[v, k, n, 5], xdev(dev),
            )

    def to_workers(v, k, stage, out, into, val):
        val = val.astype(BF16)
        for h in range(2):
            out[v, k, h * 4 : (h + 1) * 4] = val[:, h * hm : (h + 1) * hm].reshape(4, lane, hm)
        for i in wpeers:
            send(
                out.at[v, k, i], into.at[v, k, w],
                c_send.at[v, k, stage, i], c_recv.at[v, k, stage, w], wdev(i),
            )
        into[v, k, w] = out[v, k, w]

    def scan_first(v, k, val):
        to_workers(v, k, 0, shift, group_in, val)

    def order(v, n):
        return range(n) if v == 0 else range(n - 1, -1, -1)

    def worker_lanes():
        return pl.ds(pl.multiple_of(lax.div(w, 4) * hm, 128), hm)

    def scan_second(v, k):
        for i in wpeers:
            arrive(group_in.at[v, k, i], c_send.at[v, k, 0, i], c_recv.at[v, k, 0, i], wdev(i))
        total = None
        for i in order(v, NW):
            new = group_in[v, k, i].astype(F32)
            total = new if total is None else total * rate_group[i, 0:1, worker_lanes()] + new
        zone_in[v, k, z] = total.astype(BF16)
        for i in zpeers:
            send(
                zone_in.at[v, k, z], zone_in.at[v, k, z],
                c_send.at[v, k, 1, i], c_recv.at[v, k, 1, z], zdev(i),
            )

    def scan_third(v, k):
        for i in zpeers:
            arrive(zone_in.at[v, k, i], c_send.at[v, k, 1, i], c_recv.at[v, k, 1, i], zdev(i))
        for i in wpeers:
            arrive(base_in.at[v, k, i], c_send.at[v, k, 2, i], c_recv.at[v, k, 2, i], wdev(i))
        state = jnp.zeros((lane, hm), F32)
        for i in order(v, NZ):
            ahead = (i < z) if v == 0 else (i > z)
            new = state * rate_zone[i, 0:1, worker_lanes()] + zone_in[v, k, i].astype(F32)
            state = jnp.where(ahead, new, state)
        for i in order(v, NW):
            grown = state * rate_group[i, 1:2, worker_lanes()] if v == 0 else state
            reply[v, k, i] = (base_in[v, k, i].astype(F32) + grown).astype(BF16)
            state = state * rate_group[i, 0:1, worker_lanes()] + group_in[v, k, i].astype(F32)
        for d, t in enumerate(xpeers):
            for i in wpeers + [w]:
                send(
                    reply.at[v, k, i], late_in.at[v, k, x, w],
                    l_send.at[v, k, 1 + d, i], a_recv.at[v, k, x], (z * NW + i, t),
                )
        for i in wpeers:
            send(
                reply.at[v, k, i], late_in.at[v, k, x, w],
                l_send.at[v, k, 0, i], l_recv.at[v, k, 0, w], wdev(i),
            )
        late_in[v, k, x, w] = reply[v, k, w]

    def expand(v, k, n):
        t = (left, right, oppo, x)[n]
        if n == 3:
            for i in wpeers:
                arrive(late_in.at[v, k, x, i], l_send.at[v, k, 0, i], l_recv.at[v, k, 0, i], wdev(i))
            first = early[v, k]
        else:
            if n == 2:
                for m, back in ((0, left), (1, right)):
                    at = pl.ds(m * half, half)
                    arrive(early_in.at[v, k, 2, at], x_send.at[v, k, m, 5], x_recv.at[v, k, m, 5], xdev(back))
            arrive(late_in.at[v, k, t], l_send.at[v, k, 1, 0], a_recv.at[v, k, t], xdev(t))
            first = early_in[v, k, n]
        last = jnp.concatenate([late_in[v, k, t, h * 4 : (h + 1) * 4].reshape(hc, hm) for h in range(2)], axis=1)
        grown = first.astype(F32) + last.astype(F32) * coef[t, 1:2, :]
        if v == 0:
            val = jnp.concatenate([last, grown.astype(BF16)], axis=0)
            new = mm(val, S[:, block(t)], NT)
        else:
            low = (grown * coef[t, 2:3, :]).astype(BF16)
            high = (last.astype(F32) * coef[t, 3:4, :]).astype(BF16)
            val = jnp.concatenate([low, high], axis=0)
            new = mm(val, A[block(t), :], NN)
        acc[k] = new if n == 3 else acc[k] + new

    def expand_own(v, k):
        if s_copies:
            s_copies.pop().wait()
        expand(v, k, 3)

    quarter = 2 * hc // NX

    def sensors_first(k):
        for s in range(2):
            r = mm(acc[k, s * hc : (s + 1) * hc].astype(BF16), E[s], NN).astype(BF16)
            read_out[k, 2 * s : 2 * s + 2] = r.reshape(2, quarter, r.shape[-1])
        for i in xpeers:
            send(read_out.at[k, i], read_in.at[k, x], q_send.at[k, 0, i], q_recv.at[k, 0, x], xdev(i))
        read_in[k, x] = read_out[k, x]

    def sensors_second(k):
        for i in xpeers:
            arrive(read_in.at[k, i], q_send.at[k, 0, i], q_recv.at[k, 0, i], xdev(i))
        total = read_in[k, 0].astype(F32)
        for i in range(1, NX):
            total = total + read_in[k, i].astype(F32)
        weight = weights_ref[pl.ds(lax.div(x, 2), 1), :]
        wread[k, x] = (total * weight).astype(BF16)
        for i in xpeers:
            send(wread.at[k, x], wread.at[k, x], q_send.at[k, 1, i], q_recv.at[k, 1, x], xdev(i))

    def sensors_third(k):
        for i in xpeers:
            arrive(wread.at[k, i], q_send.at[k, 1, i], q_recv.at[k, 1, i], xdev(i))
        for s in range(2):
            r = wread[k, 2 * s : 2 * s + 2].reshape(hc, wread.shape[-1])
            adj[k, s * hc : (s + 1) * hc] = mm(r, E[s], NT).astype(BF16)

    def finish(k):
        for s in range(2):
            at = s * cols + k * hc
            out_ref[at : at + hc] = -disp_ref[s : s + 1, :] * acc[k, s * hc : (s + 1) * hc]

    steps = {
        "INC": build_incidence, "BAR": entered, "Z": along, "COEF1": coefficients_first, "COEF2": coefficients_second,
        "RATE1": rates_first, "RATE2": rates_second, "RATE3": rates_third,
        "P": project, "OPP": rs_opp, "MID": rs_mid, "END": rs_end, "AG2": early_second,
        "SC2": scan_second, "CAR": scan_third, "EXP": expand_own, "EXQ": expand,
        "SEN1": sensors_first, "SEN2": sensors_second, "ADJ": sensors_third, "OUT": finish,
    }
    for name in ORDER:
        if name in steps:
            steps[name]()
            continue
        if name[:2] == "FL":
            flush(int(name[2:]))
            continue
        stem = name[:1] if name[0] in "PZ" else name[:4] if name[:3] == "SEN" else name[:3]
        steps[stem](*(int(d) for d in name[len(stem) :]))
    flush(0)


def chain(directions, pivot, transfer, disp, pairs, weights, analysis, synthesis):
    dofs, _, cols = directions.shape
    rows = 2 * cols
    modes = analysis.shape[0]
    sensors = pairs.shape[2]
    vm = pltpu.VMEM
    dma = pltpu.SemaphoreType.DMA
    hc = cols // NU
    hm = dofs // 2
    lane = 2 * hc // NW
    small = (directions, pivot, transfer, disp, pairs, weights)
    scratch = [vm(a.shape, a.dtype) for a in small] + [
        vm((rows, dofs), BF16),
        vm((modes, dofs), BF16),
        vm((dofs, modes), BF16),
        vm((2, dofs, sensors), BF16),
        vm((NU, 2 * hc, dofs), F32),
        vm((NU, 4, 2 * hc, dofs), F32),
        vm((NU, hc, dofs), F32),
        vm((2, NU, 2, 2, hc // 2, dofs), BF16),
        vm((2, NU, 2, 2, hc // 2, dofs), BF16),
        vm((2, NU, 2, 2, hc, dofs), BF16),
        vm((2, NU, 2, 2, hc, dofs), BF16),
        vm((2, NU, hc, dofs), BF16),
        vm((2, NU, 3, hc, dofs), BF16),
        vm((2, NU, NX, NW, lane, hm), BF16),
        vm((2, NU, NW, lane, hm), BF16),
        vm((2, NU, NW, lane, hm), BF16),
        vm((2, NU, NW, lane, hm), BF16),
        vm((2, NU, NW, lane, hm), BF16),
        vm((2, NU, NZ, lane, hm), BF16),
        vm((2, NU, NW, lane, hm), BF16),
        vm((NX, 8, dofs), F32),
        vm((NW, 8, dofs), F32),
        vm((NZ, 8, dofs), F32),
        vm((NU, NX, 2 * hc // NX, sensors), BF16),
        vm((NU, NX, 2 * hc // NX, sensors), BF16),
        vm((NU, NX, 2 * hc // NX, sensors), BF16),
        vm((NU, 2 * hc, dofs), BF16),
        pltpu.SemaphoreType.REGULAR((3, 2)),
        dma((6,)), dma((4,)), dma((1,)),
        dma((2, NU, 2, 6)), dma((2, NU, 2, 6)),
        dma((NX,)), dma((NX,)),
        dma((2, NU, NX, NW)), dma((2, NU, 1, NW)), dma((2, NU, NX)),
        dma((2, NU, 3, 8)), dma((2, NU, 3, 8)),
        dma((2, 8)), dma((2, 8)),
        dma((NU, 2, 4)), dma((NU, 2, 4)),
    ]
    in_vmem = pl.BlockSpec(memory_space=pltpu.VMEM)
    in_hbm = pl.BlockSpec(memory_space=pl.ANY)
    return pl.pallas_call(
        kernel,
        out_shape=jax.ShapeDtypeStruct((rows, dofs), F32),
        in_specs=[in_hbm] * 8,
        out_specs=in_vmem,
        scratch_shapes=scratch,
        compiler_params=pltpu.CompilerParams(
            collective_id=0, has_side_effects=True, vmem_limit_bytes=56 * 1024 * 1024
        ),
        cost_estimate=pl.CostEstimate(
            flops=8 * rows * modes * dofs, bytes_accessed=4 * modes * dofs, transcendentals=0
        ),
        name="chain",
    )(directions, pivot, transfer, disp, pairs, weights, analysis, synthesis)


def local(synthesis, analysis, pivot, transfer, displacement, directions, sensor_pairs, sensor_weights):
    dofs, storeys, columns = directions.shape
    pairs = sensor_pairs.transpose(0, 2, 1)
    out = chain(directions, pivot, transfer, displacement, pairs, sensor_weights, analysis, synthesis)
    return out.reshape(storeys, columns, dofs).transpose(2, 0, 1)


def solution(mesh):
    return jax.shard_map(
        local,
        mesh=mesh,
        in_specs=(
            P("inner", None),
            P(None, "inner"),
            P("storey", "inner"),
            P("storey", "inner"),
            P("storey", "inner"),
            P("inner", "storey", None),
            P("storey", None, None),
            P("storey", None),
        ),
        out_specs=P("inner", "storey", None),
        check_vma=False,
    )
```

```python
import jax
import jax.numpy as jnp
from jax import lax
from jax.experimental import pallas as pl
from jax.experimental.pallas import tpu as pltpu
from jax.sharding import PartitionSpec as P

MESH = pl.DeviceIdType.MESH
F32 = jnp.float32
BF16 = jnp.bfloat16

NX = 4
NW = 8
NZ = 8
NU = 2

NN = (((1,), (0,)), ((), ()))
NT = (((1,), (1,)), ((), ()))

ORDER = (
    "BAR", "P000", "OPP000", "P012", "Z0", "P003", "OPP001", "P010", "OPP011", "OPP010", "P001", "P002", "RATE1",
    "Z1", "P013", "P011", "INC", "Z2", "MID000", "MID001", "Z3", "RATE2", "MID011", "MID010", "COEF1", "END000",
    "END001", "RATE3", "END010", "SC200", "END011", "AG200", "SC201", "AG201", "CAR00", "CAR01", "COEF2", "FL80",
    "EXQ002", "EXQ001", "EXQ000", "EXP00", "SEN10", "EXQ012", "EXQ011", "EXQ010", "EXP01", "SEN11", "SEN20",
    "SEN21", "FL12", "ADJ0", "P100", "OPP100", "P101", "P102", "P103", "OPP101", "ADJ1", "P110", "OPP110", "P113",
    "P112", "MID100", "OPP111", "P111", "MID101", "MID110", "END100", "MID111", "FL24", "END101", "SC210", "END110",
    "END111", "AG210", "FL40", "SC211", "CAR10", "AG211", "CAR11", "FL66", "EXQ102", "EXQ101", "EXQ100", "EXP10",
    "OUT0", "FL31", "EXQ112", "EXQ111", "EXQ110", "EXP11", "OUT1",
)


def mm(a, b, dims):
    return lax.dot_general(a, b, dims, preferred_element_type=F32)


def kernel(
    directions_hbm, pivot_hbm, transfer_hbm, disp_hbm, pairs_hbm, weights_hbm, analysis_hbm, synthesis_hbm,
    out_hbm,
    directions_ref, pivot_ref, transfer_ref, disp_ref, pairs_ref, weights_ref, load_ref,
    result, A, S, E, acc, part, keep, opp_out, opp_in, mid_out, mid_in, early, early_in, late_in,
    shift, group_in, base, base_in, zone_in, reply, coef, rate_group, rate_zone,
    read_out, read_in, wread, adj,
    o_sem, z_sem, in_sem, a_sem, s_sem, x_send, x_recv, k_send, k_recv, l_send, l_recv, a_recv,
    c_send, c_recv, r_send, r_recv, q_send, q_recv,
):
    storey = lax.axis_index("storey")
    x = lax.axis_index("inner")
    z = lax.div(storey, NW)
    w = lax.rem(storey, NW)
    dofs, _, cols = directions_ref.shape
    rows = 2 * cols
    hc = cols // NU
    half = hc // 2
    lane = 2 * hc // NW
    hm = dofs // 2
    right, left, oppo = lax.rem(x + 1, NX), lax.rem(x + 3, NX), lax.rem(x + 2, NX)
    pending = []
    results = []

    def xdev(i):
        return (storey, i)

    def wdev(i):
        return (z * NW + i, x)

    def zdev(i):
        return (i * NW + w, x)

    def remote(src, dst, ssem, rsem, dev):
        return pltpu.make_async_remote_copy(
            src_ref=src, dst_ref=dst, send_sem=ssem, recv_sem=rsem, device_id=dev, device_id_type=MESH
        )

    def send(src, dst, ssem, rsem, dev):
        c = remote(src, dst, ssem, rsem, dev)
        c.start()
        pending.append(c)

    def flush(keep):
        while len(pending) > keep:
            pending.pop(0).wait_send()

    def arrive(dst, ssem, rsem, dev):
        remote(dst, dst, ssem, rsem, dev).wait_recv()

    def peers(me, n):
        far_first = sorted(range(1, n), key=lambda d: -min(d, n - d))
        return [lax.rem(me + d, n) for d in far_first]

    xpeers, wpeers, zpeers = [oppo, right, left], peers(w, NW), peers(z, NZ)

    def block(t):
        return pl.ds(pl.multiple_of(t * dofs, 128), dofs)

    barrier = pltpu.get_barrier_semaphore()
    znext = (lax.rem(z + 1, NZ), lax.rem(z + NZ - 1, NZ))
    for dev in [xdev(i) for i in xpeers] + [wdev(i) for i in wpeers] + [zdev(i) for i in znext]:
        pl.semaphore_signal(barrier, inc=1, device_id=dev, device_id_type=MESH)

    def entered():
        pl.semaphore_wait(barrier, NX + NW)

    def along(r):
        for n in range(2):
            if r > 0:
                pl.semaphore_wait(z_sem.at[r - 1, n], 1)
            if r < 3:
                pl.semaphore_signal(z_sem.at[r, n], inc=1, device_id=zdev(znext[n]), device_id_type=MESH)

    def fetch(src, dst, sem):
        c = pltpu.make_async_copy(src, dst, sem)
        c.start()
        return c

    targets = (oppo, right, left, x)
    small = [fetch(directions_hbm, directions_ref, in_sem.at[0]), fetch(disp_hbm, disp_ref, in_sem.at[1])]
    a_copies = {0: fetch(analysis_hbm.at[block(targets[0]), :], A.at[block(targets[0]), :], a_sem.at[0])}
    others = ((pivot_hbm, pivot_ref), (transfer_hbm, transfer_ref), (pairs_hbm, pairs_ref), (weights_hbm, weights_ref))
    more = [fetch(src, dst, in_sem.at[2 + n]) for n, (src, dst) in enumerate(others)]
    for j in (1, 2, 3):
        a_copies[j] = fetch(analysis_hbm.at[block(targets[j]), :], A.at[block(targets[j]), :], a_sem.at[j])
    s_copies = [fetch(synthesis_hbm, S, s_sem.at[0])]

    for c in small:
        c.wait()
    for b in range(0, dofs, 128):
        both = directions_ref[b : b + 128].astype(F32)
        for s in range(2):
            turned = jnp.transpose(both[:, s, :], (1, 0))
            load_ref[s * cols : (s + 1) * cols, b : b + 128] = (-disp_ref[s : s + 1, b : b + 128] * turned).astype(BF16)
    for c in more:
        c.wait()

    t0, t1 = transfer_ref[0:1, :], transfer_ref[1:2, :]
    p0, p1 = pivot_ref[0:1, :], pivot_ref[1:2, :]
    for n, row in enumerate((t0, t1, p0, p1, t0, t1, p0, p1)):
        coef[x, n : n + 1] = row

    def coefficients_first():
        for i in xpeers:
            send(coef.at[x], coef.at[x], k_send.at[i], k_recv.at[x], xdev(i))

    def coefficients_second():
        for i in xpeers:
            arrive(coef.at[i], k_send.at[i], k_recv.at[i], xdev(i))

    def rates_first():
        rate_group[w, 0:1] = t0 * t1
        rate_group[w, 1:2] = t0
        rate_group[w, 2:8] = jnp.broadcast_to(t0, (6, dofs))
        for i in wpeers:
            send(rate_group.at[w], rate_group.at[w], r_send.at[0, i], r_recv.at[0, w], wdev(i))

    def rates_second():
        for i in wpeers:
            arrive(rate_group.at[i], r_send.at[0, i], r_recv.at[0, i], wdev(i))
        total = rate_group[0]
        for i in range(1, NW):
            total = total * rate_group[i]
        rate_zone[z] = total
        for i in zpeers:
            send(rate_zone.at[z], rate_zone.at[z], r_send.at[1, i], r_recv.at[1, z], zdev(i))

    def rates_third():
        for i in zpeers:
            arrive(rate_zone.at[i], r_send.at[1, i], r_recv.at[1, i], zdev(i))

    def build_incidence():
        sensors = pairs_ref.shape[2]
        for s in range(2):
            upper = pairs_ref[s, 0:1, :] - x * dofs
            lower = pairs_ref[s, 1:2, :] - x * dofs
            for b in range(0, dofs, 128):
                ids = lax.broadcasted_iota(jnp.int32, (128, sensors), 0) + b
                e = jnp.where(ids == upper, 1.0, 0.0) - jnp.where(ids == lower, 1.0, 0.0)
                E[s, b : b + 128] = e.astype(BF16)

    def project(v, k, j):
        t = targets[j]
        if v == 0:
            if j in a_copies:
                a_copies.pop(j).wait()
            val = jnp.concatenate([load_ref[s * cols + k * hc : s * cols + (k + 1) * hc, :] for s in range(2)], axis=0)
            part[k, j] = mm(val, A[block(t), :], NT)
        else:
            part[k, j] = mm(adj[k], S[:, block(t)], NN)

    def term(v, k, q, j, lo=0, n=hc):
        low = part[k, j, lo : lo + n]
        high = part[k, j, hc + lo : hc + lo + n]
        if v == 0:
            return high if q == 1 else low
        return high if q == 1 else low + high * coef[targets[j], 1:2, :]

    def rs_opp(v, k, q):
        for n, dev in ((0, right), (1, left)):
            opp_out[v, k, q, n] = term(v, k, q, 0, n * half, half).astype(BF16)
            send(
                opp_out.at[v, k, q, n], opp_in.at[v, k, q, n],
                x_send.at[v, k, q, n], x_recv.at[v, k, q, n], xdev(dev),
            )

    def rs_mid(v, k, q):
        for n, dev, back in ((0, right, left), (1, left, right)):
            arrive(opp_in.at[v, k, q, n], x_send.at[v, k, q, n], x_recv.at[v, k, q, n], xdev(back))
            own, other = n * half, (1 - n) * half
            mine = term(v, k, q, 1 + n, own, half) + opp_in[v, k, q, n].astype(F32)
            mid_out[v, k, q, n, own : own + half] = mine.astype(BF16)
            mid_out[v, k, q, n, other : other + half] = term(v, k, q, 1 + n, other, half).astype(BF16)
            send(
                mid_out.at[v, k, q, n], mid_in.at[v, k, q, n],
                x_send.at[v, k, q, 2 + n], x_recv.at[v, k, q, 2 + n], xdev(dev),
            )

    def rs_end(v, k, q):
        for n, back in ((0, left), (1, right)):
            arrive(mid_in.at[v, k, q, n], x_send.at[v, k, q, 2 + n], x_recv.at[v, k, q, 2 + n], xdev(back))
        total = term(v, k, q, 3) + mid_in[v, k, q, 0].astype(F32) + mid_in[v, k, q, 1].astype(F32)
        if v == 0:
            if q == 0:
                keep[k] = total * p0
            else:
                total = total * p1
                scan_first(v, k, keep[k] * t1 + total)
                early_first(v, k, total)
                to_workers(v, k, 2, base, base_in, keep[k])
        else:
            if q == 0:
                keep[k] = total
                scan_first(v, k, total * t0)
            else:
                early_first(v, k, keep[k] - total * t1)
                to_workers(v, k, 2, base, base_in, total)

    def early_first(v, k, val):
        early[v, k] = val.astype(BF16)
        for n, dev in ((0, right), (1, left)):
            send(early.at[v, k], early_in.at[v, k, n], x_send.at[v, k, n, 4], x_recv.at[v, k, n, 4], xdev(dev))

    def early_second(v, k):
        for n, dev, back in ((0, right, left), (1, left, right)):
            arrive(early_in.at[v, k, n], x_send.at[v, k, n, 4], x_recv.at[v, k, n, 4], xdev(back))
            at = pl.ds(n * half, half)
            send(
                early_in.at[v, k, n, at], early_in.at[v, k, 2, at],
                x_send.at[v, k, n, 5], x_recv.at[v, k, n, 5], xdev(dev),
            )

    def to_workers(v, k, stage, out, into, val):
        val = val.astype(BF16)
        for h in range(2):
            out[v, k, h * 4 : (h + 1) * 4] = val[:, h * hm : (h + 1) * hm].reshape(4, lane, hm)
        for i in wpeers:
            send(
                out.at[v, k, i], into.at[v, k, w],
                c_send.at[v, k, stage, i], c_recv.at[v, k, stage, w], wdev(i),
            )
        into[v, k, w] = out[v, k, w]

    def scan_first(v, k, val):
        to_workers(v, k, 0, shift, group_in, val)

    def order(v, n):
        return range(n) if v == 0 else range(n - 1, -1, -1)

    def worker_lanes():
        return pl.ds(pl.multiple_of(lax.div(w, 4) * hm, 128), hm)

    def scan_second(v, k):
        for i in wpeers:
            arrive(group_in.at[v, k, i], c_send.at[v, k, 0, i], c_recv.at[v, k, 0, i], wdev(i))
        total = None
        for i in order(v, NW):
            new = group_in[v, k, i].astype(F32)
            total = new if total is None else total * rate_group[i, 0:1, worker_lanes()] + new
        zone_in[v, k, z] = total.astype(BF16)
        for i in zpeers:
            send(
                zone_in.at[v, k, z], zone_in.at[v, k, z],
                c_send.at[v, k, 1, i], c_recv.at[v, k, 1, z], zdev(i),
            )

    def scan_third(v, k):
        for i in zpeers:
            arrive(zone_in.at[v, k, i], c_send.at[v, k, 1, i], c_recv.at[v, k, 1, i], zdev(i))
        for i in wpeers:
            arrive(base_in.at[v, k, i], c_send.at[v, k, 2, i], c_recv.at[v, k, 2, i], wdev(i))
        state = jnp.zeros((lane, hm), F32)
        for i in order(v, NZ):
            ahead = (i < z) if v == 0 else (i > z)
            new = state * rate_zone[i, 0:1, worker_lanes()] + zone_in[v, k, i].astype(F32)
            state = jnp.where(ahead, new, state)
        for i in order(v, NW):
            grown = state * rate_group[i, 1:2, worker_lanes()] if v == 0 else state
            reply[v, k, i] = (base_in[v, k, i].astype(F32) + grown).astype(BF16)
            state = state * rate_group[i, 0:1, worker_lanes()] + group_in[v, k, i].astype(F32)
        for d, t in enumerate(xpeers):
            for i in wpeers + [w]:
                send(
                    reply.at[v, k, i], late_in.at[v, k, x, w],
                    l_send.at[v, k, 1 + d, i], a_recv.at[v, k, x], (z * NW + i, t),
                )
        for i in wpeers:
            send(
                reply.at[v, k, i], late_in.at[v, k, x, w],
                l_send.at[v, k, 0, i], l_recv.at[v, k, 0, w], wdev(i),
            )
        late_in[v, k, x, w] = reply[v, k, w]

    def expand(v, k, n):
        if s_copies:
            s_copies.pop().wait()
        t = (left, right, oppo, x)[n]
        if n == 3:
            for i in wpeers:
                arrive(late_in.at[v, k, x, i], l_send.at[v, k, 0, i], l_recv.at[v, k, 0, i], wdev(i))
            first = early[v, k]
        else:
            if n == 2:
                for m, back in ((0, left), (1, right)):
                    at = pl.ds(m * half, half)
                    arrive(early_in.at[v, k, 2, at], x_send.at[v, k, m, 5], x_recv.at[v, k, m, 5], xdev(back))
            arrive(late_in.at[v, k, t], l_send.at[v, k, 1, 0], a_recv.at[v, k, t], xdev(t))
            first = early_in[v, k, n]
        last = jnp.concatenate([late_in[v, k, t, h * 4 : (h + 1) * 4].reshape(hc, hm) for h in range(2)], axis=1)
        grown = first.astype(F32) + last.astype(F32) * coef[t, 1:2, :]
        if v == 0:
            val = jnp.concatenate([last, grown.astype(BF16)], axis=0)
            new = mm(val, S[:, block(t)], NT)
        else:
            low = (grown * coef[t, 2:3, :]).astype(BF16)
            high = (last.astype(F32) * coef[t, 3:4, :]).astype(BF16)
            val = jnp.concatenate([low, high], axis=0)
            new = mm(val, A[block(t), :], NN)
        acc[k] = new if n == 2 else acc[k] + new

    def expand_own(v, k):
        expand(v, k, 3)

    quarter = 2 * hc // NX

    def sensors_first(k):
        for s in range(2):
            r = mm(acc[k, s * hc : (s + 1) * hc].astype(BF16), E[s], NN).astype(BF16)
            read_out[k, 2 * s : 2 * s + 2] = r.reshape(2, quarter, r.shape[-1])
        for i in xpeers:
            send(read_out.at[k, i], read_in.at[k, x], q_send.at[k, 0, i], q_recv.at[k, 0, x], xdev(i))
        read_in[k, x] = read_out[k, x]

    def sensors_second(k):
        for i in xpeers:
            arrive(read_in.at[k, i], q_send.at[k, 0, i], q_recv.at[k, 0, i], xdev(i))
        total = read_in[k, 0].astype(F32)
        for i in range(1, NX):
            total = total + read_in[k, i].astype(F32)
        weight = weights_ref[pl.ds(lax.div(x, 2), 1), :]
        wread[k, x] = (total * weight).astype(BF16)
        for i in xpeers:
            send(wread.at[k, x], wread.at[k, x], q_send.at[k, 1, i], q_recv.at[k, 1, x], xdev(i))

    def sensors_third(k):
        for i in xpeers:
            arrive(wread.at[k, i], q_send.at[k, 1, i], q_recv.at[k, 1, i], xdev(i))
        for s in range(2):
            r = wread[k, 2 * s : 2 * s + 2].reshape(hc, wread.shape[-1])
            adj[k, s * hc : (s + 1) * hc] = mm(r, E[s], NT).astype(BF16)

    def finish(k):
        for s in range(2):
            at = pl.ds(s * cols + k * hc, hc)
            result[at] = -disp_ref[s : s + 1, :] * acc[k, s * hc : (s + 1) * hc]
            results.append(fetch(result.at[at], out_hbm.at[at], o_sem.at[k, s]))

    steps = {
        "INC": build_incidence, "BAR": entered, "Z": along, "COEF1": coefficients_first, "COEF2": coefficients_second,
        "RATE1": rates_first, "RATE2": rates_second, "RATE3": rates_third,
        "P": project, "OPP": rs_opp, "MID": rs_mid, "END": rs_end, "AG2": early_second,
        "SC2": scan_second, "CAR": scan_third, "EXP": expand_own, "EXQ": expand,
        "SEN1": sensors_first, "SEN2": sensors_second, "ADJ": sensors_third, "OUT": finish,
    }
    for name in ORDER:
        if name in steps:
            steps[name]()
            continue
        if name[:2] == "FL":
            flush(int(name[2:]))
            continue
        stem = name[:1] if name[0] in "PZ" else name[:4] if name[:3] == "SEN" else name[:3]
        steps[stem](*(int(d) for d in name[len(stem) :]))
    flush(0)
    for c in results:
        c.wait()


def chain(directions, pivot, transfer, disp, pairs, weights, analysis, synthesis):
    dofs, _, cols = directions.shape
    rows = 2 * cols
    modes = analysis.shape[0]
    sensors = pairs.shape[2]
    vm = pltpu.VMEM
    dma = pltpu.SemaphoreType.DMA
    hc = cols // NU
    hm = dofs // 2
    lane = 2 * hc // NW
    small = (directions, pivot, transfer, disp, pairs, weights)
    scratch = [vm(a.shape, a.dtype) for a in small] + [
        vm((rows, dofs), BF16),
        vm((rows, dofs), F32),
        vm((modes, dofs), BF16),
        vm((dofs, modes), BF16),
        vm((2, dofs, sensors), BF16),
        vm((NU, 2 * hc, dofs), F32),
        vm((NU, 4, 2 * hc, dofs), F32),
        vm((NU, hc, dofs), F32),
        vm((2, NU, 2, 2, hc // 2, dofs), BF16),
        vm((2, NU, 2, 2, hc // 2, dofs), BF16),
        vm((2, NU, 2, 2, hc, dofs), BF16),
        vm((2, NU, 2, 2, hc, dofs), BF16),
        vm((2, NU, hc, dofs), BF16),
        vm((2, NU, 3, hc, dofs), BF16),
        vm((2, NU, NX, NW, lane, hm), BF16),
        vm((2, NU, NW, lane, hm), BF16),
        vm((2, NU, NW, lane, hm), BF16),
        vm((2, NU, NW, lane, hm), BF16),
        vm((2, NU, NW, lane, hm), BF16),
        vm((2, NU, NZ, lane, hm), BF16),
        vm((2, NU, NW, lane, hm), BF16),
        vm((NX, 8, dofs), F32),
        vm((NW, 8, dofs), F32),
        vm((NZ, 8, dofs), F32),
        vm((NU, NX, 2 * hc // NX, sensors), BF16),
        vm((NU, NX, 2 * hc // NX, sensors), BF16),
        vm((NU, NX, 2 * hc // NX, sensors), BF16),
        vm((NU, 2 * hc, dofs), BF16),
        dma((NU, 2)), pltpu.SemaphoreType.REGULAR((3, 2)),
        dma((6,)), dma((4,)), dma((1,)),
        dma((2, NU, 2, 6)), dma((2, NU, 2, 6)),
        dma((NX,)), dma((NX,)),
        dma((2, NU, NX, NW)), dma((2, NU, 1, NW)), dma((2, NU, NX)),
        dma((2, NU, 3, 8)), dma((2, NU, 3, 8)),
        dma((2, 8)), dma((2, 8)),
        dma((NU, 2, 4)), dma((NU, 2, 4)),
    ]
    in_hbm = pl.BlockSpec(memory_space=pl.ANY)
    return pl.pallas_call(
        kernel,
        out_shape=jax.ShapeDtypeStruct((rows, dofs), F32),
        in_specs=[in_hbm] * 8,
        out_specs=in_hbm,
        scratch_shapes=scratch,
        compiler_params=pltpu.CompilerParams(
            collective_id=0, has_side_effects=True, vmem_limit_bytes=56 * 1024 * 1024
        ),
        cost_estimate=pl.CostEstimate(
            flops=8 * rows * modes * dofs, bytes_accessed=4 * modes * dofs, transcendentals=0
        ),
        name="chain",
    )(directions, pivot, transfer, disp, pairs, weights, analysis, synthesis)


def local(synthesis, analysis, pivot, transfer, displacement, directions, sensor_pairs, sensor_weights):
    dofs, storeys, columns = directions.shape
    pairs = sensor_pairs.transpose(0, 2, 1)
    out = chain(directions, pivot, transfer, displacement, pairs, sensor_weights, analysis, synthesis)
    return out.reshape(storeys, columns, dofs).transpose(2, 0, 1)


def solution(mesh):
    return jax.shard_map(
        local,
        mesh=mesh,
        in_specs=(
            P("inner", None),
            P(None, "inner"),
            P("storey", "inner"),
            P("storey", "inner"),
            P("storey", "inner"),
            P("inner", "storey", None),
            P("storey", None, None),
            P("storey", None),
        ),
        out_specs=P("inner", "storey", None),
        check_vma=False,
    )
```
